32 devices in a mesh: seq: 4 (over x, core), chan: 8 (over z, y).
Axes of the slice: x: 2, y: 2, z: 4, core: 2. Of those that a mesh axis runs over, the one named last changes fastest.
Arguments:
- tokens: bfloat16 [512, 8192], P('seq', 'chan'), may hold values from -6 to 6
- in_weight: bfloat16 [8192, 3, 8192], P(None, None, 'chan'), may hold values from -0.0625 to 0.0625
- long_filter: float32 [512, 8192], P('seq', 'chan'), may hold values from -1 to 1
- grad_out: bfloat16 [512, 8192], P('seq', 'chan'), may hold values from -6 to 6
Outputs:
- gated_out: bfloat16 [512, 8192], P('seq', 'chan')
- grad_proj: bfloat16 [512, 3, 8192], P('seq', None, 'chan')
- grad_filter: float32 [512, 8192], P('seq', 'chan')
The draws below stay inside these ranges and needn't reach their ends.
All inputs are finite; a program needn't handle non-finite values.
Results may differ from the reference program's by a relative error of at most 0.0064.
Values may be sent and summed in bfloat16 or wider, within the bound.
No kernel may reach another device: no remote copies, remote signals or barrier semaphores. Data moves between devices by JAX's collectives and lax.ppermute only.
A program may use at most 192 MiB of HBM per device.

```python
import jax
import jax.numpy as jnp

D = 8192
SEQ = 512


def draw_long_filter(key, part):
    noise_key, rate_key = jax.random.split(key)
    filter_taps = jax.random.truncated_normal(noise_key, -4.0, 4.0, (SEQ, D), jnp.float32)
    low_log = jnp.log(30.0)
    high_log = jnp.log(4.0 * SEQ)
    decay_span = jnp.exp(jax.random.uniform(rate_key, (1, D), jnp.float32, low_log, high_log))
    steps_pos = jnp.arange(SEQ, dtype=jnp.float32)[:, None]
    return filter_taps * jnp.exp(-steps_pos / decay_span) / jnp.sqrt(jnp.minimum(decay_span, 1.0 * SEQ))


def block_levels(key, dims, pieces, smallest, high):
    loudness = 1.0
    for position, shards_of in pieces:
        heights = jax.random.uniform(jax.random.fold_in(jax.random.fold_in(key, 6), position), (shards_of,), jnp.float32, smallest / len(pieces), high / len(pieces))
        loudness = loudness * jnp.repeat(jnp.exp(heights), dims[position] // shards_of).reshape((-1,) + (1,) * (len(dims) - 1 - position))
    return loudness


def centred(own_key, dims, scale, most, pieces=(), held_as=jnp.bfloat16):
    result = scale * jax.random.normal(own_key, dims, jnp.float32)
    if pieces:
        result = result * block_levels(own_key, dims, pieces, -0.22, 0.18)
    return jnp.clip(result, -most, most).astype(held_as)


def setup_inputs(seed: int = 0) -> dict:
    key_list = jax.random.split(jax.random.key(seed), 5)
    return {
        "tokens": centred(key_list[0], (SEQ, D), 1.0, 6.0, ((0, 4), (1, 8))),
        "in_weight": centred(key_list[1], (D, 3, D), D ** -0.5, 0.0625, ((2, 8),)),
        "long_filter": draw_long_filter(jax.random.fold_in(key_list[4], 71), 0),
        "grad_out": centred(key_list[3], (SEQ, D), 1.0, 6.0, ((0, 4), (1, 8))),
    }


def reference(tokens, in_weight, long_filter, grad_out):
    projection = jnp.dot(tokens, in_weight.reshape(D, 3 * D), preferred_element_type=jnp.float32)
    projection = projection.astype(jnp.bfloat16).reshape(SEQ, 3, D)
    gate_in = projection[:, 0, :].astype(jnp.float32)
    gate_out = projection[:, 1, :].astype(jnp.float32)
    values = projection[:, 2, :].astype(jnp.float32)
    grad_dense = grad_out.astype(jnp.float32)
    source = gate_in * values
    grad_conv = grad_dense * gate_out
    padded = 2 * SEQ
    spec_source = jnp.fft.rfft(source, n=padded, axis=0)
    spec_filter = jnp.fft.rfft(long_filter, n=padded, axis=0)
    spec_grad = jnp.fft.rfft(grad_conv, n=padded, axis=0)
    conv_out = jnp.fft.irfft(spec_source * spec_filter, n=padded, axis=0)[:SEQ]
    grad_source = jnp.fft.irfft(jnp.conj(spec_filter) * spec_grad, n=padded, axis=0)[:SEQ]
    grad_filter = jnp.fft.irfft(jnp.conj(spec_source) * spec_grad, n=padded, axis=0)[:SEQ]
    gated_out = (gate_out * conv_out).astype(jnp.bfloat16)
    grad_proj = jnp.stack([grad_source * values, grad_dense * conv_out, grad_source * gate_in], axis=1)
    return gated_out, grad_proj.astype(jnp.bfloat16), grad_filter.astype(jnp.float32)
```

```python
import functools

import jax
import jax.numpy as jnp
import numpy as np
from jax import lax
from jax.experimental import pallas as pl
from jax.experimental.pallas import tpu as pltpu
from jax.sharding import PartitionSpec as P

BF16 = jnp.bfloat16
F32 = jnp.float32


def dot(a, b):
    return jnp.dot(a, b, preferred_element_type=F32)


def divisor(size, most):
    tile = min(size, most)
    while size % tile:
        tile //= 2
    return tile


def params(mebibytes):
    return pltpu.CompilerParams(vmem_limit_bytes=mebibytes * 1024 * 1024)


def mebibytes_for(size):
    return max(8, -(-size // 2**20) + 4)


def ring_order(size):
    evens = list(range(0, size, 2))
    return evens + [index + 1 for index in reversed(evens)]


def ring_pairs(size):
    order = ring_order(size)
    return [(order[i], order[(i + 1) % size]) for i in range(size)]


def ring_owners(size):
    order = ring_order(size)
    table = np.zeros((size, size), np.int32)
    for place, index in enumerate(order):
        steps = [0] + [sign * step for step in range(1, size // 2) for sign in (-1, 1)] + [size // 2]
        table[index] = [order[(place + step) % size] for step in steps]
    return table


def sequence_owners(size):
    table = np.zeros((size, size), np.int32)
    for index in range(size):
        chips = [(index + size - 2 * distance) % size for distance in range(1, size // 2)]
        table[index] = [index, index ^ 1] + chips + [chip ^ 1 for chip in chips]
    return table


def in_vmem(array):
    return pltpu.with_memory_space_constraint(array, pltpu.VMEM)


VMEM = pl.BlockSpec(memory_space=pltpu.VMEM)
SMEM = pl.BlockSpec(memory_space=pltpu.SMEM)
ANY = pl.BlockSpec(memory_space=pl.ANY)


def blocks_kernel(owners, first, fresh, place_ref, *refs):
    first_refs, refs = (refs[:2], refs[2:]) if first else ((), refs)
    total_ref, refs = (None, refs) if fresh else (refs[0], refs[1:])
    x_ref, source, out_ref, next_ref, held, sems = refs
    depth = x_ref.shape[1]
    copies = []
    for slot, target in enumerate((held, next_ref)):
        start = pl.multiple_of(place_ref[owners[slot]] * depth, depth)
        copies.append([])
        for j in range(3):
            copy = pltpu.make_async_copy(
                source.at[j, pl.ds(start, depth)], target.at[j], sems.at[slot, j]
            )
            copy.start()
            copies[slot].append(copy)
    values = [None if fresh else total_ref[j] for j in range(3)]
    if first:
        for j in range(3):
            part = dot(first_refs[0][...], first_refs[1][j])
            values[j] = part if fresh else values[j] + part
            out_ref[j] = values[j]
    for j in range(3):
        copies[0][j].wait()
        part = dot(x_ref[...], held[j])
        out_ref[j] = out_ref[j] + part if first else (part if fresh else values[j] + part)
    for copy in copies[1]:
        copy.wait()


def add_blocks(places, owners, total, first, x, weight):
    rows, depth = x.shape
    width = weight.shape[2]
    operands = [places, *(first or ())]
    aliases = {}
    if total is not None:
        aliases = {len(operands): 0}
        operands.append(total)
    operands += [x, weight]
    block = (3, depth, width)
    size = 2 * int(np.prod(block)) + 16 * rows * width + 8 * rows * depth
    return pl.pallas_call(
        functools.partial(blocks_kernel, owners, first is not None, total is None),
        in_specs=[SMEM] + [VMEM] * (len(operands) - 2) + [ANY],
        out_specs=[VMEM] * 2,
        out_shape=[jax.ShapeDtypeStruct((3, rows, width), F32), pltpu.VMEM(block, BF16)],
        scratch_shapes=[pltpu.VMEM(block, BF16), pltpu.SemaphoreType.DMA((2, 3))],
        input_output_aliases=aliases,
        compiler_params=params(mebibytes_for(size)),
        cost_estimate=pl.CostEstimate(
            flops=12 * rows * depth * width, bytes_accessed=12 * depth * width, transcendentals=0
        ),
        name="add_blocks",
    )(*operands)


def last_kernel(chunks, total_ref, grad_ref, x_ref, weight_ref, proj_ref, whole_ref, *chunk_refs):
    width = grad_ref.shape[1] // chunks
    for chunk in range(chunks):
        columns = slice(chunk * width, (chunk + 1) * width)
        streams = []
        for j in range(3):
            value = total_ref[j, :, columns] + dot(x_ref[...], weight_ref[j, :, columns])
            value = value.astype(BF16)
            proj_ref[j, :, columns] = value
            streams.append(value.astype(F32))
        source = (streams[0] * streams[2]).astype(BF16)
        grad = (grad_ref[:, columns].astype(F32) * streams[1]).astype(BF16)
        for ref, place in ((whole_ref, columns), (chunk_refs[chunk], slice(None))):
            ref[0, :, place] = source
            ref[1, :, place] = grad


def last_block(total, grad_out, x, weights, chunks):
    rows, width = grad_out.shape
    depth = x.shape[1]
    size = 40 * rows * width + 4 * rows * depth
    return pl.pallas_call(
        functools.partial(last_kernel, chunks),
        in_specs=[VMEM] * 4,
        out_specs=[VMEM] * (2 + chunks),
        out_shape=[pltpu.VMEM((3, rows, width), BF16), pltpu.VMEM((2, rows, width), BF16)]
        + [pltpu.VMEM((2, rows, width // chunks), BF16)] * chunks,
        compiler_params=params(mebibytes_for(size)),
        cost_estimate=pl.CostEstimate(
            flops=6 * rows * depth * width, bytes_accessed=2**20, transcendentals=0
        ),
        name="last_block",
    )(total, grad_out, x, in_vmem(weights))


def transform_table(length):
    steps = np.arange(length)
    turns = np.outer(2 * steps + 1, steps) % (4 * length)
    angle = turns * (np.pi / (2 * length))
    table = np.concatenate([np.cos(angle), -np.sin(angle)], axis=0).astype(np.float32)
    return jnp.asarray(table.astype(jnp.bfloat16))


def conv_kernel(chunk, final, near, far, first, where_ref, table_ref, back_ref, grad_ref, proj_ref, *refs):
    count = near + far
    tap_refs, pair_refs, refs = refs[:count], refs[count : 2 * count], refs[2 * count :]
    before_refs, refs = (refs[:3], refs[3:]) if chunk else ((), refs)
    held, sems = refs[-2:]
    result_refs, refs = refs[-5:-2], refs[:-5]
    out_refs = refs[-3:]
    gated, gproj, gfilt = result_refs
    rows, width = gated.shape
    columns = slice(chunk * width, (chunk + 1) * width)
    bins = table_ref.shape[0] // 2

    def write(refs, number, slot):
        place = pl.ds(number * width, width)
        copies = [
            pltpu.make_async_copy(refs[0], out_refs[0].at[:, place], sems.at[slot, 0]),
            pltpu.make_async_copy(refs[1], out_refs[1].at[:, :, place], sems.at[slot, 1]),
            pltpu.make_async_copy(refs[2], out_refs[2].at[:, place], sems.at[slot, 2]),
        ]
        return copies

    copies = write(before_refs, chunk - 1, 0) if chunk else []
    for copy in copies:
        copy.start()
    for block in range(count):
        place = pl.ds(pl.multiple_of(where_ref[first + block] * rows, 128), rows)
        taken = columns if block < near else slice(None)
        held[place, :width] = pair_refs[block][0, :, taken]
        held[place, width : 2 * width] = pair_refs[block][1, :, taken]
        held[place, 2 * width :] = tap_refs[block][:, columns].astype(BF16)

    def spectrum(signal):
        both = dot(table_ref[...], held[:, signal * width : (signal + 1) * width])
        return both[:bins], both[bins:]

    def back(real, imag):
        return dot(back_ref[...], jnp.concatenate([real.astype(BF16), imag.astype(BF16)], axis=0))

    src_re, src_im = spectrum(0)
    grad_re, grad_im = spectrum(1)
    filt_re, filt_im = spectrum(2)
    gfilt[...] = back(src_re * grad_re + src_im * grad_im, src_re * grad_im - src_im * grad_re)
    conv_out = back(src_re * filt_re - src_im * filt_im, src_re * filt_im + src_im * filt_re)
    grad_source = back(filt_re * grad_re + filt_im * grad_im, filt_re * grad_im - filt_im * grad_re)
    gated[...] = (proj_ref[1, :, columns].astype(F32) * conv_out).astype(BF16)
    gproj[0] = (grad_source * proj_ref[2, :, columns].astype(F32)).astype(BF16)
    gproj[1] = (grad_ref[:, columns].astype(F32) * conv_out).astype(BF16)
    gproj[2] = (grad_source * proj_ref[0, :, columns].astype(F32)).astype(BF16)
    if final:
        mine = write(result_refs, chunk, 1)
        for copy in mine:
            copy.start()
        copies = copies + mine
    for copy in copies:
        copy.wait()


def convolve(places, first, table, back, grad_out, proj, taps, near, far, before, outs, chunk, final):
    rows, width = grad_out.shape
    length = table.shape[1]
    chunk_width = far[0].shape[2]
    operands = [places, table, back, grad_out, proj, *taps, *near, *far, *before]
    in_specs = [SMEM] + [VMEM] * (len(operands) - 1)
    out_specs, out_shape, aliases = [], [], {}
    if chunk or final:
        out_specs = [ANY] * 3
        out_shape = [
            jax.ShapeDtypeStruct((rows, width), BF16),
            jax.ShapeDtypeStruct((3, rows, width), BF16),
            jax.ShapeDtypeStruct((rows, width), F32),
        ]
    if outs:
        aliases = {len(operands) + i: i for i in range(3)}
        in_specs += [ANY] * 3
        operands += outs
    results = [((rows, chunk_width), BF16), ((3, rows, chunk_width), BF16), ((rows, chunk_width), F32)]
    scratch = [pltpu.VMEM(*result) for result in results] if final else []
    if not final:
        out_specs += [VMEM] * 3
        out_shape += [pltpu.VMEM(*result) for result in results]
    size = 60 * length * chunk_width + 2**22
    out = pl.pallas_call(
        functools.partial(conv_kernel, chunk, final, len(near), len(far), first),
        in_specs=in_specs,
        out_specs=out_specs,
        out_shape=out_shape,
        scratch_shapes=scratch
        + [
            pltpu.VMEM((length, 3 * chunk_width), BF16),
            pltpu.SemaphoreType.DMA((2, 3)),
        ],
        input_output_aliases=aliases,
        compiler_params=params(mebibytes_for(size)),
        cost_estimate=pl.CostEstimate(
            flops=6 * (table.size + 2 * rows * length) * chunk_width,
            bytes_accessed=2**20,
            transcendentals=0,
        ),
        name="convolve",
    )(*operands)
    out = list(out)
    outs = [out.pop(0) for _ in range(3)] if chunk or final else []
    return outs, out


def to_other_core(value, groups):
    return lax.ppermute(value, "seq", [(i, i ^ 1) for i in range(groups)])


def from_other_chips(value, groups):
    return [
        lax.ppermute(value, "seq", [(i, (i + 2 * d) % groups) for i in range(groups)])
        for d in range(1, groups // 2)
    ]


def per_device(tokens, in_weight, long_filter, grad_out):
    rows, width = long_filter.shape
    depth = tokens.shape[1]
    groups = lax.axis_size("seq")
    chans = lax.axis_size("chan")
    seq_index = lax.axis_index("seq")
    chan_index = lax.axis_index("chan")
    length = rows * groups
    weight = jnp.transpose(in_weight, (1, 0, 2))

    owners = np.concatenate(
        [
            np.repeat(sequence_owners(groups), chans, axis=0),
            np.tile(ring_owners(chans), (groups, 1)),
        ],
        axis=1,
    )
    places = lax.dynamic_index_in_dim(
        jnp.asarray(owners), seq_index * chans + chan_index, 0, keepdims=False
    )
    forward = ring_pairs(chans)
    reverse = [(b, a) for a, b in forward]
    steps = chans // 2

    up, down = tokens, tokens
    total, first, x = None, None, tokens
    for step in range(1, steps + 1):
        next_up = lax.ppermute(up, "chan", forward)
        if step < steps:
            next_down = lax.ppermute(down, "chan", reverse)
        if step == 1:
            taps = [long_filter] + from_other_chips(long_filter, groups)
            taps += [to_other_core(block, groups) for block in taps]
        now = 0 if step == 1 else 2 * step - 2
        total, weights = add_blocks(
            places, (groups + now, groups + 2 * step - 1), total, first, x, weight
        )
        if step < steps:
            up, down, total = lax.optimization_barrier((next_up, next_down, total))
            first, x = (up, in_vmem(weights)), down

    table = transform_table(length)
    back = lax.dynamic_slice(table, (0, seq_index * rows), (2 * length, rows))
    back = jnp.transpose(back) * jnp.asarray(1.0 / length, BF16)
    taps = [taps[0], taps[groups // 2]] + taps[1 : groups // 2] + taps[groups // 2 + 1 :]

    chunks = width // divisor(width, 256)
    proj, pair, *pieces = last_block(total, grad_out, next_up, weights, chunks)
    near = [pair, to_other_core(pair, groups)]
    fars = [from_other_chips(piece, groups) for piece in pieces]
    outs, before = [], []
    for chunk in range(chunks):
        far = fars[chunk]
        if chunk >= 2:
            *far, before[0] = lax.optimization_barrier((*far, before[0]))
        fars[chunk] = far + [to_other_core(block, groups) for block in far]
        if chunk:
            outs, before = convolve(
                places, 0, table, back, grad_out, proj, taps, near, fars[chunk - 1], before, outs, chunk - 1, False
            )
    outs, _ = convolve(
        places, 0, table, back, grad_out, proj, taps, near, fars[-1], before, outs, chunks - 1, True
    )
    gated_out, grad_proj, grad_filter = outs
    return gated_out, jnp.transpose(grad_proj, (1, 0, 2)), grad_filter


def solution(mesh):
    in_specs = (P("seq", "chan"), P(None, None, "chan"), P("seq", "chan"), P("seq", "chan"))
    out_specs = (P("seq", "chan"), P("seq", None, "chan"), P("seq", "chan"))
    return jax.shard_map(
        per_device, mesh=mesh, in_specs=in_specs, out_specs=out_specs, check_vma=False
    )
```

```python
import functools

import jax
import jax.numpy as jnp
import numpy as np
from jax import lax
from jax.experimental import pallas as pl
from jax.experimental.pallas import tpu as pltpu
from jax.sharding import PartitionSpec as P

BF16 = jnp.bfloat16
F32 = jnp.float32


def dot(a, b):
    return jnp.dot(a, b, preferred_element_type=F32)


def divisor(size, most):
    tile = min(size, most)
    while size % tile:
        tile //= 2
    return tile


def params(mebibytes):
    return pltpu.CompilerParams(vmem_limit_bytes=mebibytes * 1024 * 1024)


def mebibytes_for(size):
    return max(8, -(-size // 2**20) + 4)


def ring_order(size):
    evens = list(range(0, size, 2))
    return evens + [index + 1 for index in reversed(evens)]


def ring_pairs(size):
    order = ring_order(size)
    return [(order[i], order[(i + 1) % size]) for i in range(size)]


def ring_owner(device, chans, offset):
    index = lax.rem(device, chans)
    half = lax.div(index, 2)
    position = jnp.where(lax.rem(index, 2) == 0, half, chans - 1 - half)
    position = lax.rem(position + (offset + chans), chans)
    return jnp.where(position < chans // 2, 2 * position, 2 * (chans - 1 - position) + 1)


def sequence_owner(device, chans, groups, distance):
    return lax.rem(lax.div(device, chans) + (groups - 2 * distance), groups)


def in_vmem(array):
    return pltpu.with_memory_space_constraint(array, pltpu.VMEM)


VMEM = pl.BlockSpec(memory_space=pltpu.VMEM)
SMEM = pl.BlockSpec(memory_space=pltpu.SMEM)
ANY = pl.BlockSpec(memory_space=pl.ANY)
HBM = pl.BlockSpec(memory_space=pltpu.HBM)


def blocks_kernel(chans, offsets, first, fresh, own, device_ref, *refs):
    first_refs, refs = (refs[:2], refs[2:]) if first else ((), refs)
    total_ref, refs = (None, refs) if fresh else (refs[0], refs[1:])
    x_ref, source, out_ref, next_ref, held, sems, *own_refs = refs
    depth = x_ref.shape[1]
    if own:
        own_x, own_sem = own_refs
        own_copy = pltpu.make_async_copy(x_ref, own_x, own_sem)
        own_copy.start()
        x_ref = own_x
    copies = []
    for slot, target in enumerate((held, next_ref)):
        start = pl.multiple_of(ring_owner(device_ref[0], chans, offsets[slot]) * depth, depth)
        copies.append(
            pltpu.make_async_copy(source.at[:, pl.ds(start, depth)], target, sems.at[slot])
        )
        copies[slot].start()
    values = [None if fresh else total_ref[j] for j in range(3)]
    if first:
        for j in range(3):
            part = dot(first_refs[0][...], first_refs[1][j])
            values[j] = part if fresh else values[j] + part
            out_ref[j] = values[j]
    if own:
        own_copy.wait()
    copies[0].wait()
    for j in range(3):
        part = dot(x_ref[...], held[j])
        out_ref[j] = out_ref[j] + part if first else (part if fresh else values[j] + part)
    copies[1].wait()


def add_blocks(device, chans, offsets, total, first, x, weight):
    rows, depth = x.shape
    width = weight.shape[2]
    own = first is None
    operands = [device, *(first or ())]
    aliases = {}
    if total is not None:
        aliases = {len(operands): 0}
        operands.append(total)
    operands += [x, weight]
    block = (3, depth, width)
    size = 2 * int(np.prod(block)) + 16 * rows * width + 8 * rows * depth
    scratch = [pltpu.VMEM(block, BF16), pltpu.SemaphoreType.DMA((2,))]
    if own:
        scratch += [pltpu.VMEM((rows, depth), BF16), pltpu.SemaphoreType.DMA]
    return pl.pallas_call(
        functools.partial(blocks_kernel, chans, offsets, not own, total is None, own),
        in_specs=[SMEM] + [VMEM] * (len(operands) - 3) + [ANY if own else VMEM, ANY],
        out_specs=[VMEM] * 2,
        out_shape=[jax.ShapeDtypeStruct((3, rows, width), F32), pltpu.VMEM(block, BF16)],
        scratch_shapes=scratch,
        input_output_aliases=aliases,
        compiler_params=params(mebibytes_for(size)),
        cost_estimate=pl.CostEstimate(
            flops=12 * rows * depth * width, bytes_accessed=12 * depth * width, transcendentals=0
        ),
        name="add_blocks",
    )(*operands)


def last_kernel(cuts, total_ref, grad_ref, x_ref, weight_ref, proj_ref, whole_ref, *chunk_refs):
    for chunk_ref, columns in zip(chunk_refs, cuts):
        streams = []
        for j in range(3):
            value = total_ref[j, :, columns] + dot(x_ref[...], weight_ref[j, :, columns])
            value = value.astype(BF16)
            proj_ref[j, :, columns] = value
            streams.append(value.astype(F32))
        source = (streams[0] * streams[2]).astype(BF16)
        grad = (grad_ref[:, columns].astype(F32) * streams[1]).astype(BF16)
        for ref, place in ((whole_ref, columns), (chunk_ref, slice(None))):
            ref[0, :, place] = source
            ref[1, :, place] = grad


def last_block(total, grad_out, x, weights, cuts):
    rows, width = grad_out.shape
    depth = x.shape[1]
    size = 40 * rows * width + 4 * rows * depth
    return pl.pallas_call(
        functools.partial(last_kernel, cuts),
        in_specs=[VMEM] * 4,
        out_specs=[VMEM] * (2 + len(cuts)),
        out_shape=[pltpu.VMEM((3, rows, width), BF16), pltpu.VMEM((2, rows, width), BF16)]
        + [pltpu.VMEM((2, rows, cut.stop - cut.start), BF16) for cut in cuts],
        compiler_params=params(mebibytes_for(size)),
        cost_estimate=pl.CostEstimate(
            flops=6 * rows * depth * width, bytes_accessed=2**20, transcendentals=0
        ),
        name="last_block",
    )(total, grad_out, x, in_vmem(weights))


def transform_table(length):
    steps = np.arange(length)
    turns = np.outer(2 * steps + 1, steps) % (4 * length)
    angle = turns * (np.pi / (2 * length))
    table = np.concatenate([np.cos(angle), -np.sin(angle)], axis=0).astype(np.float32)
    return jnp.asarray(table.astype(jnp.bfloat16))


def chip_rows(owner, ref, other_ref, columns):
    first = lax.rem(owner, 2) == 0
    signals = []
    for signal in range(2):
        mine, others = ref[signal, :, columns], other_ref[signal, :, columns]
        signals.append(
            jnp.concatenate([jnp.where(first, mine, others), jnp.where(first, others, mine)], axis=0)
        )
    return jnp.concatenate(signals, axis=1)


def chip_table(table_ref, owner, rows):
    return table_ref[:, pl.ds(pl.multiple_of(owner // 2 * 2 * rows, 256), 2 * rows)]


def spectra_kernel(chans, groups, device_ref, table_ref, *refs):
    tap_refs, (own_ref, other_ref, filt_ref, near_ref, back_ref, taps) = refs[:groups], refs[groups:]
    rows, width = tap_refs[0].shape
    tile = divisor(width, 256)
    chips = groups // 2
    for number, ref in enumerate(tap_refs):
        owner = sequence_owner(device_ref[0], chans, groups, number % chips)
        if number >= chips:
            owner = owner + 1 - 2 * lax.rem(owner, 2)
        taps[pl.ds(pl.multiple_of(owner * rows, 128), rows)] = ref[...]
    for start in range(0, width, tile):
        columns = slice(start, start + tile)
        filt_ref[:, columns] = dot(table_ref[...], taps[:, columns])
    owner = sequence_owner(device_ref[0], chans, groups, 0)
    length = table_ref.shape[1]
    mine = table_ref[:, pl.ds(pl.multiple_of(owner * rows, 128), rows)]
    back_ref[...] = (mine.astype(F32).T * (1.0 / length)).astype(BF16)
    table = chip_table(table_ref, owner, rows)
    for start in range(0, width, tile):
        held = chip_rows(owner, own_ref, other_ref, slice(start, start + tile))
        near_ref[:, 2 * start : 2 * start + 2 * tile] = dot(table, held)


def spectra(device, chans, table, taps, pair, other_pair):
    rows, width = taps[0].shape
    bins, length = table.shape
    size = 2 * table.size + 4 * length * width + 40 * rows * width + 2**21
    return pl.pallas_call(
        functools.partial(spectra_kernel, chans, len(taps)),
        in_specs=[SMEM] + [VMEM] * (3 + len(taps)),
        out_specs=[VMEM] * 3,
        out_shape=[
            pltpu.VMEM((bins, width), F32),
            pltpu.VMEM((bins, 2 * width), F32),
            pltpu.VMEM((rows, bins), BF16),
        ],
        scratch_shapes=[pltpu.VMEM((length, width), BF16)],
        compiler_params=params(mebibytes_for(size)),
        cost_estimate=pl.CostEstimate(flops=2**20, bytes_accessed=2**16, transcendentals=0),
        name="spectra",
    )(device, table, *taps, pair, other_pair)


def conv_kernel(chans, groups, pieces, first, tile, aliased, device_ref, *refs):
    chips = groups // 2 - 1
    table_ref, back_ref, grad_ref, proj_ref, filt_ref, near_ref, *refs = refs
    count = 2 * chips * pieces
    far_refs, refs = refs[:count], refs[count + 3 * aliased :]
    gated_out, gproj_out, gfilt_out, gated, gproj, gfilt, sems = refs
    rows, width = gated.shape
    bins = table_ref.shape[0] // 2
    owners = [sequence_owner(device_ref[0], chans, groups, chip + 1) for chip in range(chips)]
    piece_width = width // pieces
    copies = []
    for start in range(0, width, tile):
        here = slice(start, start + tile)
        there = slice(first + start, first + start + tile)
        pairs = slice(2 * (first + start), 2 * (first + start) + 2 * tile)
        both = near_ref[:, pairs]
        piece, offset = divmod(start, piece_width)
        for chip, owner in enumerate(owners):
            held = chip_rows(
                owner,
                far_refs[chip * pieces + piece],
                far_refs[(chips + chip) * pieces + piece],
                slice(offset, offset + tile),
            )
            both = both + dot(chip_table(table_ref, owner, rows), held)
        src_re, src_im = both[:bins, :tile], both[bins:, :tile]
        grad_re, grad_im = both[:bins, tile:], both[bins:, tile:]
        filt_re, filt_im = filt_ref[:bins, there], filt_ref[bins:, there]
        real = [
            src_re * filt_re - src_im * filt_im,
            filt_re * grad_re + filt_im * grad_im,
            src_re * grad_re + src_im * grad_im,
        ]
        imag = [
            src_re * filt_im + src_im * filt_re,
            filt_re * grad_im - filt_im * grad_re,
            src_re * grad_im - src_im * grad_re,
        ]
        products = jnp.concatenate(
            [
                jnp.concatenate([re.astype(BF16), im.astype(BF16)], axis=0)
                for re, im in zip(real, imag)
            ],
            axis=1,
        )
        result = dot(back_ref[...], products)
        conv_out, grad_source = result[:, :tile], result[:, tile : 2 * tile]
        gfilt[:, here] = result[:, 2 * tile :]
        gated[:, here] = (proj_ref[1, :, there].astype(F32) * conv_out).astype(BF16)
        gproj[0, :, here] = (grad_source * proj_ref[2, :, there].astype(F32)).astype(BF16)
        gproj[1, :, here] = (grad_ref[:, there].astype(F32) * conv_out).astype(BF16)
        gproj[2, :, here] = (grad_source * proj_ref[0, :, there].astype(F32)).astype(BF16)
        number = start // tile
        copies += [
            pltpu.make_async_copy(gated.at[:, here], gated_out.at[:, there], sems.at[number, 0]),
            pltpu.make_async_copy(gproj.at[:, :, here], gproj_out.at[:, :, there], sems.at[number, 1]),
            pltpu.make_async_copy(gfilt.at[:, here], gfilt_out.at[:, there], sems.at[number, 2]),
        ]
        for copy in copies[-3:]:
            copy.start()
    for copy in copies:
        copy.wait()


def convolve(device, chans, groups, table, back, grad_out, proj, filt, near, far, pieces, outs, cut):
    rows, width = grad_out.shape
    bins, length = table.shape
    chunk_width = cut.stop - cut.start
    chips = groups // 2 - 1
    tile = divisor(chunk_width, 256)
    operands = [device, table, back, grad_out, proj, filt, near, *far]
    in_specs = [SMEM] + [VMEM] * (len(operands) - 1)
    aliases = {}
    if outs:
        aliases = {len(operands) + i: i for i in range(3)}
        in_specs += [ANY] * 3
        operands += outs
    size = 48 * length * tile + 20 * chips * rows * chunk_width + 2 * table.size + 2**22
    return pl.pallas_call(
        functools.partial(conv_kernel, chans, groups, pieces, cut.start, tile, bool(outs)),
        in_specs=in_specs,
        out_specs=[ANY] * 3,
        out_shape=[
            jax.ShapeDtypeStruct((rows, width), BF16),
            jax.ShapeDtypeStruct((3, rows, width), BF16),
            jax.ShapeDtypeStruct((rows, width), F32),
        ],
        scratch_shapes=[
            pltpu.VMEM((rows, chunk_width), BF16),
            pltpu.VMEM((3, rows, chunk_width), BF16),
            pltpu.VMEM((rows, chunk_width), F32),
            pltpu.SemaphoreType.DMA((chunk_width // tile, 3)),
        ],
        input_output_aliases=aliases,
        compiler_params=params(mebibytes_for(size)),
        cost_estimate=pl.CostEstimate(flops=2**20, bytes_accessed=2**16, transcendentals=0),
        name="convolve",
    )(*operands)


def to_other_core(value, groups):
    return lax.ppermute(value, "seq", [(i, i ^ 1) for i in range(groups)])


def from_other_chips(value, groups):
    return [
        lax.ppermute(value, "seq", [(i, (i + 2 * d) % groups) for i in range(groups)])
        for d in range(1, groups // 2)
    ]


def per_device(tokens, in_weight, long_filter, grad_out):
    rows, width = long_filter.shape
    depth = tokens.shape[1]
    groups = lax.axis_size("seq")
    chans = lax.axis_size("chan")
    seq_index = lax.axis_index("seq")
    chan_index = lax.axis_index("chan")
    length = rows * groups
    weight = jnp.transpose(in_weight, (1, 0, 2))

    device = (seq_index * chans + chan_index)[None]
    forward = ring_pairs(chans)
    reverse = [(b, a) for a, b in forward]
    steps = chans // 2

    up, down = tokens, tokens
    total, first, x = None, None, pltpu.with_memory_space_constraint(tokens, pltpu.HBM)
    for step in range(1, steps + 1):
        next_up = lax.ppermute(up, "chan", forward)
        if step < steps:
            next_down = lax.ppermute(down, "chan", reverse)
        if step == 1:
            filt = long_filter.astype(BF16)
        if step == steps:
            taps = [filt] + from_other_chips(filt, groups)
        total, weights = add_blocks(
            device, chans, (step - 1, -step), total, first, x, weight
        )
        if step < steps:
            up, down, total, filt = lax.optimization_barrier((next_up, next_down, total, filt))
            first, x = (up, in_vmem(weights)), down
        else:
            last, total, *taps = lax.optimization_barrier((next_up, total, *taps))

    table = transform_table(length)
    edge = width // 2
    cuts = [slice(0, edge), slice(edge, width)] if edge % 256 == 0 else [slice(0, width)]
    pieces = [slice(0, edge // 2), slice(edge // 2, edge)] + cuts[1:] if len(cuts) > 1 else cuts
    proj, pair, *parts = last_block(total, grad_out, last, weights, pieces)
    fars = [from_other_chips(part, groups) for part in parts]
    filt, near, back = spectra(
        device,
        chans,
        table,
        taps + [to_other_core(block, groups) for block in taps],
        pair,
        to_other_core(pair, groups),
    )
    outs = None
    for cut in cuts:
        far = [fars.pop(0) for piece in pieces if cut.start <= piece.start < cut.stop]
        count = len(far)
        far = [block for blocks in zip(*far) for block in blocks]
        if outs:
            *far, outs[2] = lax.optimization_barrier((*far, outs[2]))
        else:
            *far, near = lax.optimization_barrier((*far, near))
        far = far + [to_other_core(block, groups) for block in far]
        outs = list(
            convolve(
                device, chans, groups, table, back, grad_out, proj, filt, near, far, count, outs, cut
            )
        )
    gated_out, grad_proj, grad_filter = outs
    return gated_out, jnp.transpose(grad_proj, (1, 0, 2)), grad_filter


def solution(mesh):
    in_specs = (P("seq", "chan"), P(None, None, "chan"), P("seq", "chan"), P("seq", "chan"))
    out_specs = (P("seq", "chan"), P("seq", None, "chan"), P("seq", "chan"))
    return jax.shard_map(
        per_device, mesh=mesh, in_specs=in_specs, out_specs=out_specs, check_vma=False
    )
```

```python
import functools

import jax
import jax.numpy as jnp
import numpy as np
from jax import lax
from jax.experimental import pallas as pl
from jax.experimental.pallas import tpu as pltpu
from jax.sharding import PartitionSpec as P

BF16 = jnp.bfloat16
F32 = jnp.float32


def dot(a, b):
    return jnp.dot(a, b, preferred_element_type=F32)


def divisor(size, most):
    tile = min(size, most)
    while size % tile:
        tile //= 2
    return tile


def params(mebibytes):
    return pltpu.CompilerParams(vmem_limit_bytes=mebibytes * 1024 * 1024)


def mebibytes_for(size):
    return max(8, -(-size // 2**20) + 4)


def ring_order(size):
    evens = list(range(0, size, 2))
    return evens + [index + 1 for index in reversed(evens)]


def ring_pairs(size):
    order = ring_order(size)
    return [(order[i], order[(i + 1) % size]) for i in range(size)]


def ring_owner(device, chans, offset):
    index = lax.rem(device, chans)
    half = lax.div(index, 2)
    position = jnp.where(lax.rem(index, 2) == 0, half, chans - 1 - half)
    position = lax.rem(position + (offset + chans), chans)
    return jnp.where(position < chans // 2, 2 * position, 2 * (chans - 1 - position) + 1)


def sequence_owner(device, chans, groups, distance):
    return lax.rem(lax.div(device, chans) + (groups - 2 * distance), groups)


def in_vmem(array):
    return pltpu.with_memory_space_constraint(array, pltpu.VMEM)


VMEM = pl.BlockSpec(memory_space=pltpu.VMEM)
SMEM = pl.BlockSpec(memory_space=pltpu.SMEM)
ANY = pl.BlockSpec(memory_space=pl.ANY)
HBM = pl.BlockSpec(memory_space=pltpu.HBM)


def blocks_kernel(chans, offsets, first, fresh, own, device_ref, *refs):
    first_refs, refs = (refs[:2], refs[2:]) if first else ((), refs)
    total_ref, refs = (None, refs) if fresh else (refs[0], refs[1:])
    x_ref, source, out_ref, next_ref, held, sems, *own_refs = refs
    depth = x_ref.shape[1]
    if own:
        own_x, own_sem = own_refs
        own_copy = pltpu.make_async_copy(x_ref, own_x, own_sem)
        own_copy.start()
        x_ref = own_x
    copies = []
    for slot, target in enumerate((held, next_ref)):
        start = pl.multiple_of(ring_owner(device_ref[0], chans, offsets[slot]) * depth, depth)
        copies.append(
            pltpu.make_async_copy(source.at[:, pl.ds(start, depth)], target, sems.at[slot])
        )
        copies[slot].start()
    values = [None if fresh else total_ref[j] for j in range(3)]
    if first:
        for j in range(3):
            part = dot(first_refs[0][...], first_refs[1][j])
            values[j] = part if fresh else values[j] + part
            out_ref[j] = values[j]
    if own:
        own_copy.wait()
    copies[0].wait()
    for j in range(3):
        part = dot(x_ref[...], held[j])
        out_ref[j] = out_ref[j] + part if first else (part if fresh else values[j] + part)
    copies[1].wait()


def add_blocks(device, chans, offsets, total, first, x, weight):
    rows, depth = x.shape
    width = weight.shape[2]
    own = first is None
    operands = [device, *(first or ())]
    aliases = {}
    if total is not None:
        aliases = {len(operands): 0}
        operands.append(total)
    operands += [x, weight]
    block = (3, depth, width)
    size = 2 * int(np.prod(block)) + 16 * rows * width + 8 * rows * depth
    scratch = [pltpu.VMEM(block, BF16), pltpu.SemaphoreType.DMA((2,))]
    if own:
        scratch += [pltpu.VMEM((rows, depth), BF16), pltpu.SemaphoreType.DMA]
    return pl.pallas_call(
        functools.partial(blocks_kernel, chans, offsets, not own, total is None, own),
        in_specs=[SMEM] + [VMEM] * (len(operands) - 3) + [ANY if own else VMEM, ANY],
        out_specs=[VMEM] * 2,
        out_shape=[jax.ShapeDtypeStruct((3, rows, width), F32), pltpu.VMEM(block, BF16)],
        scratch_shapes=scratch,
        input_output_aliases=aliases,
        compiler_params=params(mebibytes_for(size)),
        cost_estimate=pl.CostEstimate(
            flops=12 * rows * depth * width, bytes_accessed=12 * depth * width, transcendentals=0
        ),
        name="add_blocks",
    )(*operands)


def last_kernel(cuts, total_ref, grad_ref, x_ref, weight_ref, proj_ref, whole_ref, *piece_refs):
    for piece_ref, columns in zip(piece_refs, cuts):
        streams = []
        for j in range(3):
            value = total_ref[j, :, columns] + dot(x_ref[...], weight_ref[j, :, columns])
            value = value.astype(BF16)
            proj_ref[j, :, columns] = value
            streams.append(value.astype(F32))
        source = (streams[0] * streams[2]).astype(BF16)
        grad = (grad_ref[:, columns].astype(F32) * streams[1]).astype(BF16)
        for ref, place in ((whole_ref, columns), (piece_ref, slice(None))):
            ref[0, :, place] = source
            ref[1, :, place] = grad


def last_block(total, grad_out, x, weights, cuts):
    rows, width = grad_out.shape
    depth = x.shape[1]
    size = 40 * rows * width + 4 * rows * depth
    return pl.pallas_call(
        functools.partial(last_kernel, cuts),
        in_specs=[VMEM] * 4,
        out_specs=[VMEM] * (2 + len(cuts)),
        out_shape=[pltpu.VMEM((3, rows, width), BF16), pltpu.VMEM((2, rows, width), BF16)]
        + [pltpu.VMEM((2, rows, cut.stop - cut.start), BF16) for cut in cuts],
        compiler_params=params(mebibytes_for(size)),
        cost_estimate=pl.CostEstimate(
            flops=6 * rows * depth * width, bytes_accessed=2**20, transcendentals=0
        ),
        name="last_block",
    )(total, grad_out, x, in_vmem(weights))


def transform_table(length):
    steps = np.arange(length)
    turns = np.outer(2 * steps + 1, steps) % (4 * length)
    angle = turns * (np.pi / (2 * length))
    table = np.concatenate([np.cos(angle), -np.sin(angle)], axis=0).astype(np.float32)
    return jnp.asarray(table.astype(jnp.bfloat16))


def chip_rows(owner, ref, other_ref):
    first = lax.rem(owner, 2) == 0
    signals = []
    for signal in range(2):
        mine, others = ref[signal], other_ref[signal]
        signals.append(
            jnp.concatenate([jnp.where(first, mine, others), jnp.where(first, others, mine)], axis=0)
        )
    return jnp.concatenate(signals, axis=1)


def chip_table(table_ref, owner, rows):
    return table_ref[:, pl.ds(pl.multiple_of(owner // 2 * 2 * rows, 256), 2 * rows)]


def spectra_kernel(chans, groups, device_ref, table_ref, *refs):
    tap_refs, (own_ref, *other_refs) = refs[:groups], refs[groups:-4]
    filt_ref, near_ref, back_ref, taps = refs[-4:]
    rows, width = tap_refs[0].shape
    tile = divisor(width, 256)
    chips = groups // 2
    for number, ref in enumerate(tap_refs):
        owner = sequence_owner(device_ref[0], chans, groups, number % chips)
        if number >= chips:
            owner = owner + 1 - 2 * lax.rem(owner, 2)
        taps[pl.ds(pl.multiple_of(owner * rows, 128), rows)] = ref[...]
    for start in range(0, width, tile):
        columns = slice(start, start + tile)
        filt_ref[:, columns] = dot(table_ref[...], taps[:, columns])
    owner = sequence_owner(device_ref[0], chans, groups, 0)
    length = table_ref.shape[1]
    mine = table_ref[:, pl.ds(pl.multiple_of(owner * rows, 128), rows)]
    back_ref[...] = (mine.astype(F32).T * (1.0 / length)).astype(BF16)
    table = chip_table(table_ref, owner, rows)
    for start in range(0, width, tile):
        piece, offset = divmod(start, other_refs[0].shape[2])
        held = chip_rows(
            owner,
            own_ref.at[:, :, start : start + tile],
            other_refs[piece].at[:, :, offset : offset + tile],
        )
        near_ref[:, 2 * start : 2 * start + 2 * tile] = dot(table, held)


def spectra(device, chans, table, taps, pair, other_pieces):
    rows, width = taps[0].shape
    bins, length = table.shape
    size = 2 * table.size + 4 * length * width + 40 * rows * width + 2**21
    return pl.pallas_call(
        functools.partial(spectra_kernel, chans, len(taps)),
        in_specs=[SMEM] + [VMEM] * (2 + len(taps) + len(other_pieces)),
        out_specs=[VMEM] * 3,
        out_shape=[
            pltpu.VMEM((bins, width), F32),
            pltpu.VMEM((bins, 2 * width), F32),
            pltpu.VMEM((rows, bins), BF16),
        ],
        scratch_shapes=[pltpu.VMEM((length, width), BF16)],
        compiler_params=params(mebibytes_for(size)),
        cost_estimate=pl.CostEstimate(flops=2**20, bytes_accessed=2**16, transcendentals=0),
        name="spectra",
    )(device, table, *taps, pair, *other_pieces)


def conv_kernel(chans, groups, pieces, first, tile, aliased, device_ref, *refs):
    chips = groups // 2 - 1
    table_ref, back_ref, grad_ref, proj_ref, filt_ref, near_ref, *refs = refs
    count = 2 * chips * pieces
    far_refs, refs = refs[:count], refs[count + 3 * aliased :]
    gated_out, gproj_out, gfilt_out, gated, gproj, gfilt, sems = refs
    rows, width = gated.shape
    bins = table_ref.shape[0] // 2
    owners = [sequence_owner(device_ref[0], chans, groups, chip + 1) for chip in range(chips)]
    piece_width = width // pieces
    copies = []
    for start in range(0, width, tile):
        here = slice(start, start + tile)
        there = slice(first + start, first + start + tile)
        pairs = slice(2 * (first + start), 2 * (first + start) + 2 * tile)
        both = near_ref[:, pairs]
        piece, offset = divmod(start, piece_width)
        for chip, owner in enumerate(owners):
            held = chip_rows(
                owner,
                far_refs[chip * pieces + piece].at[:, :, offset : offset + tile],
                far_refs[(chips + chip) * pieces + piece].at[:, :, offset : offset + tile],
            )
            both = both + dot(chip_table(table_ref, owner, rows), held)
        src_re, src_im = both[:bins, :tile], both[bins:, :tile]
        grad_re, grad_im = both[:bins, tile:], both[bins:, tile:]
        filt_re, filt_im = filt_ref[:bins, there], filt_ref[bins:, there]
        real = [
            src_re * filt_re - src_im * filt_im,
            filt_re * grad_re + filt_im * grad_im,
            src_re * grad_re + src_im * grad_im,
        ]
        imag = [
            src_re * filt_im + src_im * filt_re,
            filt_re * grad_im - filt_im * grad_re,
            src_re * grad_im - src_im * grad_re,
        ]
        products = jnp.concatenate(
            [
                jnp.concatenate([re.astype(BF16), im.astype(BF16)], axis=0)
                for re, im in zip(real, imag)
            ],
            axis=1,
        )
        result = dot(back_ref[...], products)
        conv_out, grad_source = result[:, :tile], result[:, tile : 2 * tile]
        gfilt[:, here] = result[:, 2 * tile :]
        gated[:, here] = (proj_ref[1, :, there].astype(F32) * conv_out).astype(BF16)
        gproj[0, :, here] = (grad_source * proj_ref[2, :, there].astype(F32)).astype(BF16)
        gproj[1, :, here] = (grad_ref[:, there].astype(F32) * conv_out).astype(BF16)
        gproj[2, :, here] = (grad_source * proj_ref[0, :, there].astype(F32)).astype(BF16)
        number = start // tile
        copies += [
            pltpu.make_async_copy(gated.at[:, here], gated_out.at[:, there], sems.at[number, 0]),
            pltpu.make_async_copy(gproj.at[:, :, here], gproj_out.at[:, :, there], sems.at[number, 1]),
            pltpu.make_async_copy(gfilt.at[:, here], gfilt_out.at[:, there], sems.at[number, 2]),
        ]
        for copy in copies[-3:]:
            copy.start()
    for copy in copies:
        copy.wait()


def convolve(device, chans, groups, table, back, grad_out, proj, filt, near, far, pieces, outs, cut):
    rows, width = grad_out.shape
    bins, length = table.shape
    chunk_width = cut.stop - cut.start
    chips = groups // 2 - 1
    tile = divisor(chunk_width, 256)
    operands = [device, table, back, grad_out, proj, filt, near, *far]
    in_specs = [SMEM] + [VMEM] * (len(operands) - 1)
    aliases = {}
    if outs:
        aliases = {len(operands) + i: i for i in range(3)}
        in_specs += [ANY] * 3
        operands += outs
    size = 48 * length * tile + 20 * chips * rows * chunk_width + 2 * table.size + 2**22
    return pl.pallas_call(
        functools.partial(conv_kernel, chans, groups, pieces, cut.start, tile, bool(outs)),
        in_specs=in_specs,
        out_specs=[ANY] * 3,
        out_shape=[
            jax.ShapeDtypeStruct((rows, width), BF16),
            jax.ShapeDtypeStruct((3, rows, width), BF16),
            jax.ShapeDtypeStruct((rows, width), F32),
        ],
        scratch_shapes=[
            pltpu.VMEM((rows, chunk_width), BF16),
            pltpu.VMEM((3, rows, chunk_width), BF16),
            pltpu.VMEM((rows, chunk_width), F32),
            pltpu.SemaphoreType.DMA((chunk_width // tile, 3)),
        ],
        input_output_aliases=aliases,
        compiler_params=params(mebibytes_for(size)),
        cost_estimate=pl.CostEstimate(flops=2**20, bytes_accessed=2**16, transcendentals=0),
        name="convolve",
    )(*operands)


def to_other_core(value, groups):
    return lax.ppermute(value, "seq", [(i, i ^ 1) for i in range(groups)])


def from_other_chips(value, groups):
    return [
        lax.ppermute(value, "seq", [(i, (i + 2 * d) % groups) for i in range(groups)])
        for d in range(1, groups // 2)
    ]


def per_device(tokens, in_weight, long_filter, grad_out):
    rows, width = long_filter.shape
    depth = tokens.shape[1]
    groups = lax.axis_size("seq")
    chans = lax.axis_size("chan")
    seq_index = lax.axis_index("seq")
    chan_index = lax.axis_index("chan")
    length = rows * groups
    weight = jnp.transpose(in_weight, (1, 0, 2))

    device = (seq_index * chans + chan_index)[None]
    forward = ring_pairs(chans)
    reverse = [(b, a) for a, b in forward]
    steps = chans // 2

    up, down = tokens, tokens
    total, first, x = None, None, pltpu.with_memory_space_constraint(tokens, pltpu.HBM)
    for step in range(1, steps + 1):
        next_up = lax.ppermute(up, "chan", forward)
        if step < steps:
            next_down = lax.ppermute(down, "chan", reverse)
        if step == 1:
            filt = long_filter.astype(BF16)
        if step == steps:
            taps = [filt] + from_other_chips(filt, groups)
        total, weights = add_blocks(
            device, chans, (step - 1, -step), total, first, x, weight
        )
        if step < steps:
            up, down, total, filt = lax.optimization_barrier((next_up, next_down, total, filt))
            first, x = (up, in_vmem(weights)), down
        else:
            last, total, *taps = lax.optimization_barrier((next_up, total, *taps))

    table = transform_table(length)
    edge = width // 2
    pieces = [slice(0, edge), slice(edge, width)] if edge % 256 == 0 else [slice(0, width)]
    proj, pair, *parts = last_block(total, grad_out, last, weights, pieces)
    far = from_other_chips(pair, groups)
    taps = taps + [to_other_core(block, groups) for block in taps]
    others = [to_other_core(part, groups) for part in parts]
    filt, near, back = spectra(device, chans, table, taps, pair, others)
    *far, near = lax.optimization_barrier((*far, near))
    far = far + [to_other_core(block, groups) for block in far]
    outs = convolve(
        device, chans, groups, table, back, grad_out, proj, filt, near, far, 1, None, slice(0, width)
    )
    gated_out, grad_proj, grad_filter = outs
    return gated_out, jnp.transpose(grad_proj, (1, 0, 2)), grad_filter


def solution(mesh):
    in_specs = (P("seq", "chan"), P(None, None, "chan"), P("seq", "chan"), P("seq", "chan"))
    out_specs = (P("seq", "chan"), P("seq", None, "chan"), P("seq", "chan"))
    return jax.shard_map(
        per_device, mesh=mesh, in_specs=in_specs, out_specs=out_specs, check_vma=False
    )
```

```python
import functools

import jax
import jax.numpy as jnp
import numpy as np
from jax import lax
from jax.experimental import pallas as pl
from jax.experimental.pallas import tpu as pltpu
from jax.sharding import PartitionSpec as P

BF16 = jnp.bfloat16
F32 = jnp.float32


def dot(a, b):
    return jnp.dot(a, b, preferred_element_type=F32)


def divisor(size, most):
    tile = min(size, most)
    while size % tile:
        tile //= 2
    return tile


def params(mebibytes):
    return pltpu.CompilerParams(vmem_limit_bytes=mebibytes * 1024 * 1024)


def mebibytes_for(size):
    return max(8, -(-size // 2**20) + 4)


def ring_order(size):
    evens = list(range(0, size, 2))
    return evens + [index + 1 for index in reversed(evens)]


def ring_pairs(size):
    order = ring_order(size)
    return [(order[i], order[(i + 1) % size]) for i in range(size)]


def ring_owner(device, chans, offset):
    index = lax.rem(device, chans)
    half = lax.div(index, 2)
    position = jnp.where(lax.rem(index, 2) == 0, half, chans - 1 - half)
    position = lax.rem(position + (offset + chans), chans)
    return jnp.where(position < chans // 2, 2 * position, 2 * (chans - 1 - position) + 1)


def sequence_owner(device, chans, groups, distance):
    return lax.rem(lax.div(device, chans) + (groups - 2 * distance), groups)


def in_vmem(array):
    return pltpu.with_memory_space_constraint(array, pltpu.VMEM)


VMEM = pl.BlockSpec(memory_space=pltpu.VMEM)
SMEM = pl.BlockSpec(memory_space=pltpu.SMEM)
ANY = pl.BlockSpec(memory_space=pl.ANY)
HBM = pl.BlockSpec(memory_space=pltpu.HBM)


def blocks_kernel(chans, offsets, first, fresh, own, device_ref, *refs):
    first_refs, refs = (refs[:2], refs[2:]) if first else ((), refs)
    total_ref, refs = (None, refs) if fresh else (refs[0], refs[1:])
    x_ref, source, out_ref, next_ref, held, sems, *own_refs = refs
    depth = x_ref.shape[1]
    if own:
        own_x, own_sem = own_refs
        own_copy = pltpu.make_async_copy(x_ref, own_x, own_sem)
        own_copy.start()
        x_ref = own_x
    copies = []
    for slot, target in enumerate((held, next_ref)):
        start = pl.multiple_of(ring_owner(device_ref[0], chans, offsets[slot]) * depth, depth)
        copies.append(
            pltpu.make_async_copy(source.at[:, pl.ds(start, depth)], target, sems.at[slot])
        )
        copies[slot].start()
    values = [None if fresh else total_ref[j] for j in range(3)]
    if first:
        for j in range(3):
            part = dot(first_refs[0][...], first_refs[1][j])
            values[j] = part if fresh else values[j] + part
            out_ref[j] = values[j]
    if own:
        own_copy.wait()
    copies[0].wait()
    for j in range(3):
        part = dot(x_ref[...], held[j])
        out_ref[j] = out_ref[j] + part if first else (part if fresh else values[j] + part)
    copies[1].wait()


def add_blocks(device, chans, offsets, total, first, x, weight):
    rows, depth = x.shape
    width = weight.shape[2]
    own = first is None
    operands = [device, *(first or ())]
    aliases = {}
    if total is not None:
        aliases = {len(operands): 0}
        operands.append(total)
    operands += [x, weight]
    block = (3, depth, width)
    size = 2 * int(np.prod(block)) + 16 * rows * width + 8 * rows * depth
    scratch = [pltpu.VMEM(block, BF16), pltpu.SemaphoreType.DMA((2,))]
    if own:
        scratch += [pltpu.VMEM((rows, depth), BF16), pltpu.SemaphoreType.DMA]
    return pl.pallas_call(
        functools.partial(blocks_kernel, chans, offsets, not own, total is None, own),
        in_specs=[SMEM] + [VMEM] * (len(operands) - 3) + [ANY if own else VMEM, ANY],
        out_specs=[VMEM] * 2,
        out_shape=[jax.ShapeDtypeStruct((3, rows, width), F32), pltpu.VMEM(block, BF16)],
        scratch_shapes=scratch,
        input_output_aliases=aliases,
        compiler_params=params(mebibytes_for(size)),
        cost_estimate=pl.CostEstimate(
            flops=12 * rows * depth * width, bytes_accessed=12 * depth * width, transcendentals=0
        ),
        name="add_blocks",
    )(*operands)


def last_kernel(cuts, total_ref, grad_ref, x_ref, weight_ref, proj_ref, whole_ref, *piece_refs):
    for piece_ref, columns in zip(piece_refs, cuts):
        streams = []
        for j in range(3):
            value = total_ref[j, :, columns] + dot(x_ref[...], weight_ref[j, :, columns])
            value = value.astype(BF16)
            proj_ref[j, :, columns] = value
            streams.append(value.astype(F32))
        source = (streams[0] * streams[2]).astype(BF16)
        grad = (grad_ref[:, columns].astype(F32) * streams[1]).astype(BF16)
        for ref, place in ((whole_ref, columns), (piece_ref, slice(None))):
            ref[0, :, place] = source
            ref[1, :, place] = grad


def last_block(total, grad_out, x, weights, cuts):
    rows, width = grad_out.shape
    depth = x.shape[1]
    size = 40 * rows * width + 4 * rows * depth
    return pl.pallas_call(
        functools.partial(last_kernel, cuts),
        in_specs=[VMEM] * 4,
        out_specs=[VMEM] * (2 + len(cuts)),
        out_shape=[pltpu.VMEM((3, rows, width), BF16), pltpu.VMEM((2, rows, width), BF16)]
        + [pltpu.VMEM((2, rows, cut.stop - cut.start), BF16) for cut in cuts],
        compiler_params=params(mebibytes_for(size)),
        cost_estimate=pl.CostEstimate(
            flops=6 * rows * depth * width, bytes_accessed=2**20, transcendentals=0
        ),
        name="last_block",
    )(total, grad_out, x, in_vmem(weights))


def transform_table(length):
    steps = np.arange(length)
    turns = np.outer(2 * steps + 1, steps) % (4 * length)
    angle = turns * (np.pi / (2 * length))
    table = np.concatenate([np.cos(angle), -np.sin(angle)], axis=0).astype(np.float32)
    return jnp.asarray(table.astype(jnp.bfloat16))


def chip_rows(owner, ref, other_ref):
    first = lax.rem(owner, 2) == 0
    signals = []
    for signal in range(2):
        mine, others = ref[signal], other_ref[signal]
        signals.append(
            jnp.concatenate([jnp.where(first, mine, others), jnp.where(first, others, mine)], axis=0)
        )
    return jnp.concatenate(signals, axis=1)


def chip_table(table_ref, owner, rows):
    return table_ref[:, pl.ds(pl.multiple_of(owner // 2 * 2 * rows, 256), 2 * rows)]


def spectra_kernel(chans, groups, device_ref, table_ref, *refs):
    tap_refs, (own_ref, *other_refs) = refs[:groups], refs[groups:-4]
    filt_ref, near_ref, back_ref, taps = refs[-4:]
    rows, width = own_ref.shape[1:]
    tile = divisor(width, 256)
    chips = groups // 2
    for number, ref in enumerate(tap_refs):
        owner = sequence_owner(device_ref[0], chans, groups, number % chips)
        if number >= chips:
            owner = owner + 1 - 2 * lax.rem(owner, 2)
        taps[pl.ds(pl.multiple_of(owner * rows, 128), rows)] = ref[:rows]
    for start in range(0, width, tile):
        columns = slice(start, start + tile)
        filt_ref[:, columns] = dot(table_ref[...], taps[:, columns])
    owner = sequence_owner(device_ref[0], chans, groups, 0)
    length = table_ref.shape[1]
    mine = table_ref[:, pl.ds(pl.multiple_of(owner * rows, 128), rows)]
    back_ref[...] = (mine.astype(F32).T * (1.0 / length)).astype(BF16)
    table = chip_table(table_ref, owner, rows)
    for start in range(0, width, tile):
        piece, offset = divmod(start, other_refs[0].shape[2])
        held = chip_rows(
            owner,
            own_ref.at[:, :, start : start + tile],
            other_refs[piece].at[:, :, offset : offset + tile],
        )
        near_ref[:, 2 * start : 2 * start + 2 * tile] = dot(table, held)


def spectra(device, chans, table, taps, pair, other_pieces):
    rows, width = pair.shape[1:]
    bins, length = table.shape
    size = 2 * table.size + 4 * length * width + 40 * rows * width + 2**21
    return pl.pallas_call(
        functools.partial(spectra_kernel, chans, len(taps)),
        in_specs=[SMEM] + [VMEM] * (2 + len(taps) + len(other_pieces)),
        out_specs=[VMEM] * 3,
        out_shape=[
            pltpu.VMEM((bins, width), F32),
            pltpu.VMEM((bins, 2 * width), F32),
            pltpu.VMEM((rows, bins), BF16),
        ],
        scratch_shapes=[pltpu.VMEM((length, width), BF16)],
        compiler_params=params(mebibytes_for(size)),
        cost_estimate=pl.CostEstimate(flops=2**20, bytes_accessed=2**16, transcendentals=0),
        name="spectra",
    )(device, table, *taps, pair, *other_pieces)


def conv_kernel(chans, groups, pieces, first, tile, aliased, device_ref, *refs):
    chips = groups // 2 - 1
    table_ref, back_ref, grad_ref, proj_ref, filt_ref, near_ref, *refs = refs
    count = 2 * chips * pieces
    far_refs, refs = refs[:count], refs[count + 3 * aliased :]
    gated_out, gproj_out, gfilt_out, gated, gproj, gfilt, sems = refs
    rows, width = gated.shape
    bins = table_ref.shape[0] // 2
    owners = [sequence_owner(device_ref[0], chans, groups, chip + 1) for chip in range(chips)]
    piece_width = width // pieces
    copies = []
    for start in range(0, width, tile):
        here = slice(start, start + tile)
        there = slice(first + start, first + start + tile)
        pairs = slice(2 * (first + start), 2 * (first + start) + 2 * tile)
        both = near_ref[:, pairs]
        piece, offset = divmod(start, piece_width)
        for chip, owner in enumerate(owners):
            held = chip_rows(
                owner,
                far_refs[chip * pieces + piece].at[:, :, offset : offset + tile],
                far_refs[(chips + chip) * pieces + piece].at[:, :, offset : offset + tile],
            )
            both = both + dot(chip_table(table_ref, owner, rows), held)
        src_re, src_im = both[:bins, :tile], both[bins:, :tile]
        grad_re, grad_im = both[:bins, tile:], both[bins:, tile:]
        filt_re, filt_im = filt_ref[:bins, there], filt_ref[bins:, there]
        real = [
            src_re * filt_re - src_im * filt_im,
            filt_re * grad_re + filt_im * grad_im,
            src_re * grad_re + src_im * grad_im,
        ]
        imag = [
            src_re * filt_im + src_im * filt_re,
            filt_re * grad_im - filt_im * grad_re,
            src_re * grad_im - src_im * grad_re,
        ]
        products = jnp.concatenate(
            [
                jnp.concatenate([re.astype(BF16), im.astype(BF16)], axis=0)
                for re, im in zip(real, imag)
            ],
            axis=1,
        )
        result = dot(back_ref[...], products)
        conv_out, grad_source = result[:, :tile], result[:, tile : 2 * tile]
        gfilt[:, here] = result[:, 2 * tile :]
        gated[:, here] = (proj_ref[1, :, there].astype(F32) * conv_out).astype(BF16)
        gproj[0, :, here] = (grad_source * proj_ref[2, :, there].astype(F32)).astype(BF16)
        gproj[1, :, here] = (grad_ref[:, there].astype(F32) * conv_out).astype(BF16)
        gproj[2, :, here] = (grad_source * proj_ref[0, :, there].astype(F32)).astype(BF16)
        number = start // tile
        copies += [
            pltpu.make_async_copy(gated.at[:, here], gated_out.at[:, there], sems.at[number, 0]),
            pltpu.make_async_copy(gproj.at[:, :, here], gproj_out.at[:, :, there], sems.at[number, 1]),
            pltpu.make_async_copy(gfilt.at[:, here], gfilt_out.at[:, there], sems.at[number, 2]),
        ]
        for copy in copies[-3:]:
            copy.start()
    for copy in copies:
        copy.wait()


def convolve(device, chans, groups, table, back, grad_out, proj, filt, near, far, pieces, outs, cut):
    rows, width = grad_out.shape
    bins, length = table.shape
    chunk_width = cut.stop - cut.start
    chips = groups // 2 - 1
    tile = divisor(chunk_width, 256)
    operands = [device, table, back, grad_out, proj, filt, near, *far]
    in_specs = [SMEM] + [VMEM] * (len(operands) - 1)
    aliases = {}
    if outs:
        aliases = {len(operands) + i: i for i in range(3)}
        in_specs += [ANY] * 3
        operands += outs
    size = 48 * length * tile + 20 * chips * rows * chunk_width + 2 * table.size + 2**22
    return pl.pallas_call(
        functools.partial(conv_kernel, chans, groups, pieces, cut.start, tile, bool(outs)),
        in_specs=in_specs,
        out_specs=[ANY] * 3,
        out_shape=[
            jax.ShapeDtypeStruct((rows, width), BF16),
            jax.ShapeDtypeStruct((3, rows, width), BF16),
            jax.ShapeDtypeStruct((rows, width), F32),
        ],
        scratch_shapes=[
            pltpu.VMEM((rows, chunk_width), BF16),
            pltpu.VMEM((3, rows, chunk_width), BF16),
            pltpu.VMEM((rows, chunk_width), F32),
            pltpu.SemaphoreType.DMA((chunk_width // tile, 3)),
        ],
        input_output_aliases=aliases,
        compiler_params=params(mebibytes_for(size)),
        cost_estimate=pl.CostEstimate(flops=2**20, bytes_accessed=2**16, transcendentals=0),
        name="convolve",
    )(*operands)


def to_other_core(value, groups):
    return lax.ppermute(value, "seq", [(i, i ^ 1) for i in range(groups)])


def from_other_chips(value, groups):
    return [
        lax.ppermute(value, "seq", [(i, (i + 2 * d) % groups) for i in range(groups)])
        for d in range(1, groups // 2)
    ]


def per_device(tokens, in_weight, long_filter, grad_out):
    rows, width = long_filter.shape
    depth = tokens.shape[1]
    groups = lax.axis_size("seq")
    chans = lax.axis_size("chan")
    seq_index = lax.axis_index("seq")
    chan_index = lax.axis_index("chan")
    length = rows * groups
    weight = jnp.transpose(in_weight, (1, 0, 2))

    device = (seq_index * chans + chan_index)[None]
    forward = ring_pairs(chans)
    reverse = [(b, a) for a, b in forward]
    steps = chans // 2

    up, down = tokens, tokens
    total, first, x = None, None, pltpu.with_memory_space_constraint(tokens, pltpu.HBM)
    for step in range(1, steps + 1):
        next_up = lax.ppermute(up, "chan", forward)
        if step < steps:
            next_down = lax.ppermute(down, "chan", reverse)
        total, weights = add_blocks(
            device, chans, (step - 1, -step), total, first, x, weight
        )
        taps = []
        if step == 1:
            total, filt = lax.optimization_barrier(
                (total, jnp.concatenate([long_filter, long_filter[:16]], axis=0).astype(BF16))
            )
            filters = [filt] + from_other_chips(filt, groups)
        if step == 2:
            taps = filters
        if step < steps:
            up, down, total, *taps = lax.optimization_barrier((next_up, next_down, total, *taps))
            filters = taps or filters
            first, x = (up, in_vmem(weights)), down
        else:
            last, total = lax.optimization_barrier((next_up, total))
    taps = filters

    table = transform_table(length)
    edge = width // 2
    pieces = [slice(0, edge), slice(edge, width)] if edge % 256 == 0 else [slice(0, width)]
    proj, pair, *parts = last_block(total, grad_out, last, weights, pieces)
    far = from_other_chips(pair, groups)
    taps = taps + [to_other_core(block, groups) for block in taps]
    others = [to_other_core(part, groups) for part in parts]
    filt, near, back = spectra(device, chans, table, taps, pair, others)
    *far, near = lax.optimization_barrier((*far, near))
    far = far + [to_other_core(block, groups) for block in far]
    outs = convolve(
        device, chans, groups, table, back, grad_out, proj, filt, near, far, 1, None, slice(0, width)
    )
    gated_out, grad_proj, grad_filter = outs
    return gated_out, jnp.transpose(grad_proj, (1, 0, 2)), grad_filter


def solution(mesh):
    in_specs = (P("seq", "chan"), P(None, None, "chan"), P("seq", "chan"), P("seq", "chan"))
    out_specs = (P("seq", "chan"), P("seq", None, "chan"), P("seq", "chan"))
    return jax.shard_map(
        per_device, mesh=mesh, in_specs=in_specs, out_specs=out_specs, check_vma=False
    )
```

```python
import functools

import jax
import jax.numpy as jnp
import numpy as np
from jax import lax
from jax.experimental import pallas as pl
from jax.experimental.pallas import tpu as pltpu
from jax.sharding import PartitionSpec as P

BF16 = jnp.bfloat16
F32 = jnp.float32


def dot(a, b):
    return jnp.dot(a, b, preferred_element_type=F32)


def divisor(size, most):
    tile = min(size, most)
    while size % tile:
        tile //= 2
    return tile


def params(mebibytes):
    return pltpu.CompilerParams(vmem_limit_bytes=mebibytes * 1024 * 1024)


def mebibytes_for(size):
    return max(8, -(-size // 2**20) + 4)


def ring_order(size):
    evens = list(range(0, size, 2))
    return evens + [index + 1 for index in reversed(evens)]


def ring_pairs(size):
    order = ring_order(size)
    return [(order[i], order[(i + 1) % size]) for i in range(size)]


def ring_owner(device, chans, offset):
    index = lax.rem(device, chans)
    half = lax.div(index, 2)
    position = jnp.where(lax.rem(index, 2) == 0, half, chans - 1 - half)
    position = lax.rem(position + (offset + chans), chans)
    return jnp.where(position < chans // 2, 2 * position, 2 * (chans - 1 - position) + 1)


def sequence_owner(device, chans, groups, distance):
    return lax.rem(lax.div(device, chans) + (groups - 2 * distance), groups)


def in_vmem(array):
    return pltpu.with_memory_space_constraint(array, pltpu.VMEM)


SPARE = 16
VMEM = pl.BlockSpec(memory_space=pltpu.VMEM)
SMEM = pl.BlockSpec(memory_space=pltpu.SMEM)
ANY = pl.BlockSpec(memory_space=pl.ANY)
HBM = pl.BlockSpec(memory_space=pltpu.HBM)


def blocks_kernel(chans, offsets, first, fresh, own, device_ref, *refs):
    first_refs, refs = (refs[:2], refs[2:]) if first else ((), refs)
    total_ref, refs = (None, refs) if fresh else (refs[0], refs[1:])
    if own:
        x_ref, source, filter_ref, out_ref, next_ref, filt_ref, held, sems, *own_refs = refs
        own_x, own_filter, own_sems = own_refs
        own_copies = [
            pltpu.make_async_copy(x_ref, own_x, own_sems.at[0]),
            pltpu.make_async_copy(filter_ref, own_filter, own_sems.at[1]),
        ]
        own_copies[0].start()
        x_ref = own_x
    else:
        x_ref, source, out_ref, next_ref, held, sems = refs
    depth = x_ref.shape[1]
    copies = []
    for slot, target in enumerate((held, next_ref)):
        start = pl.multiple_of(ring_owner(device_ref[0], chans, offsets[slot]) * depth, depth)
        copies.append(
            pltpu.make_async_copy(source.at[:, pl.ds(start, depth)], target, sems.at[slot])
        )
        copies[slot].start()
    if own:
        own_copies[1].start()
    values = [None if fresh else total_ref[j] for j in range(3)]
    if first:
        for j in range(3):
            part = dot(first_refs[0][...], first_refs[1][j])
            values[j] = part if fresh else values[j] + part
            out_ref[j] = values[j]
    if own:
        own_copies[0].wait()
    copies[0].wait()
    for j in range(3):
        part = dot(x_ref[...], held[j])
        out_ref[j] = out_ref[j] + part if first else (part if fresh else values[j] + part)
    if own:
        own_copies[1].wait()
        rows = own_filter.shape[0]
        filt_ref[:rows] = own_filter[...].astype(BF16)
        filt_ref[rows:] = own_filter[: filt_ref.shape[0] - rows].astype(BF16)
    copies[1].wait()


def add_blocks(device, chans, offsets, total, first, x, weight, long_filter=None):
    rows, depth = x.shape
    width = weight.shape[2]
    own = first is None
    operands = [device, *(first or ())]
    aliases = {}
    if total is not None:
        aliases = {len(operands): 0}
        operands.append(total)
    operands += [x, weight] + [long_filter] * own
    block = (3, depth, width)
    size = 2 * int(np.prod(block)) + 16 * rows * width + 8 * rows * depth
    scratch = [pltpu.VMEM(block, BF16), pltpu.SemaphoreType.DMA((2,))]
    if own:
        size += 16 * rows * width
        scratch += [
            pltpu.VMEM((rows, depth), BF16),
            pltpu.VMEM((rows, width), F32),
            pltpu.SemaphoreType.DMA((2,)),
        ]
    return pl.pallas_call(
        functools.partial(blocks_kernel, chans, offsets, not own, total is None, own),
        in_specs=[SMEM] + ([ANY] * 3 if own else [VMEM] * (len(operands) - 2) + [ANY]),
        out_specs=[VMEM] * (2 + own),
        out_shape=[jax.ShapeDtypeStruct((3, rows, width), F32), pltpu.VMEM(block, BF16)]
        + [jax.ShapeDtypeStruct((rows + SPARE, width), BF16)] * own,
        scratch_shapes=scratch,
        input_output_aliases=aliases,
        compiler_params=params(mebibytes_for(size)),
        cost_estimate=pl.CostEstimate(
            flops=12 * rows * depth * width, bytes_accessed=12 * depth * width, transcendentals=0
        ),
        name="add_blocks",
    )(*operands)


def last_kernel(cuts, total_ref, grad_ref, x_ref, weight_ref, proj_ref, whole_ref, *piece_refs):
    for piece_ref, columns in zip(piece_refs, cuts):
        streams = []
        for j in range(3):
            value = total_ref[j, :, columns] + dot(x_ref[...], weight_ref[j, :, columns])
            value = value.astype(BF16)
            proj_ref[j, :, columns] = value
            streams.append(value.astype(F32))
        source = (streams[0] * streams[2]).astype(BF16)
        grad = (grad_ref[:, columns].astype(F32) * streams[1]).astype(BF16)
        for ref, place in ((whole_ref, columns), (piece_ref, slice(None))):
            ref[0, :, place] = source
            ref[1, :, place] = grad


def last_block(total, grad_out, x, weights, cuts):
    rows, width = grad_out.shape
    depth = x.shape[1]
    size = 40 * rows * width + 4 * rows * depth
    return pl.pallas_call(
        functools.partial(last_kernel, cuts),
        in_specs=[VMEM] * 4,
        out_specs=[VMEM] * (2 + len(cuts)),
        out_shape=[pltpu.VMEM((3, rows, width), BF16), pltpu.VMEM((2, rows, width), BF16)]
        + [pltpu.VMEM((2, rows, cut.stop - cut.start), BF16) for cut in cuts],
        compiler_params=params(mebibytes_for(size)),
        cost_estimate=pl.CostEstimate(
            flops=6 * rows * depth * width, bytes_accessed=2**20, transcendentals=0
        ),
        name="last_block",
    )(total, grad_out, x, in_vmem(weights))


def transform_table(length):
    steps = np.arange(length)
    turns = np.outer(2 * steps + 1, steps) % (4 * length)
    angle = turns * (np.pi / (2 * length))
    table = np.concatenate([np.cos(angle), -np.sin(angle)], axis=0).astype(np.float32)
    return jnp.asarray(table.astype(jnp.bfloat16))


def chip_rows(owner, ref, other_ref):
    first = lax.rem(owner, 2) == 0
    signals = []
    for signal in range(2):
        mine, others = ref[signal], other_ref[signal]
        signals.append(
            jnp.concatenate([jnp.where(first, mine, others), jnp.where(first, others, mine)], axis=0)
        )
    return jnp.concatenate(signals, axis=1)


def chip_table(table_ref, owner, rows):
    return table_ref[:, pl.ds(pl.multiple_of(owner // 2 * 2 * rows, 256), 2 * rows)]


def spectra_kernel(chans, groups, device_ref, table_ref, *refs):
    tap_refs, (own_ref, *other_refs) = refs[:groups], refs[groups:-4]
    filt_ref, near_ref, back_ref, taps = refs[-4:]
    rows, width = own_ref.shape[1:]
    tile = divisor(width, 256)
    chips = groups // 2
    for number, ref in enumerate(tap_refs):
        owner = sequence_owner(device_ref[0], chans, groups, number % chips)
        if number >= chips:
            owner = owner + 1 - 2 * lax.rem(owner, 2)
        taps[pl.ds(pl.multiple_of(owner * rows, 128), rows)] = ref[:rows]
    for start in range(0, width, tile):
        columns = slice(start, start + tile)
        filt_ref[:, columns] = dot(table_ref[...], taps[:, columns])
    owner = sequence_owner(device_ref[0], chans, groups, 0)
    length = table_ref.shape[1]
    mine = table_ref[:, pl.ds(pl.multiple_of(owner * rows, 128), rows)]
    back_ref[...] = (mine.astype(F32).T * (1.0 / length)).astype(BF16)
    table = chip_table(table_ref, owner, rows)
    for start in range(0, width, tile):
        piece, offset = divmod(start, other_refs[0].shape[2])
        held = chip_rows(
            owner,
            own_ref.at[:, :, start : start + tile],
            other_refs[piece].at[:, :, offset : offset + tile],
        )
        near_ref[:, 2 * start : 2 * start + 2 * tile] = dot(table, held)


def spectra(device, chans, table, taps, pair, other_pieces):
    rows, width = pair.shape[1:]
    bins, length = table.shape
    size = 2 * table.size + 4 * length * width + 40 * rows * width + 2**21
    return pl.pallas_call(
        functools.partial(spectra_kernel, chans, len(taps)),
        in_specs=[SMEM] + [VMEM] * (2 + len(taps) + len(other_pieces)),
        out_specs=[VMEM] * 3,
        out_shape=[
            pltpu.VMEM((bins, width), F32),
            pltpu.VMEM((bins, 2 * width), F32),
            pltpu.VMEM((rows, bins), BF16),
        ],
        scratch_shapes=[pltpu.VMEM((length, width), BF16)],
        compiler_params=params(mebibytes_for(size)),
        cost_estimate=pl.CostEstimate(flops=2**20, bytes_accessed=2**16, transcendentals=0),
        name="spectra",
    )(device, table, *taps, pair, *other_pieces)


def conv_kernel(chans, groups, pieces, first, tile, aliased, device_ref, *refs):
    chips = groups // 2 - 1
    table_ref, back_ref, grad_ref, proj_ref, filt_ref, near_ref, *refs = refs
    count = 2 * chips * pieces
    far_refs, refs = refs[:count], refs[count + 3 * aliased :]
    gated_out, gproj_out, gfilt_out, gated, gproj, gfilt, sems = refs
    rows, width = gated.shape
    bins = table_ref.shape[0] // 2
    owners = [sequence_owner(device_ref[0], chans, groups, chip + 1) for chip in range(chips)]
    piece_width = width // pieces
    copies = []
    for start in range(0, width, tile):
        here = slice(start, start + tile)
        there = slice(first + start, first + start + tile)
        pairs = slice(2 * (first + start), 2 * (first + start) + 2 * tile)
        both = near_ref[:, pairs]
        piece, offset = divmod(start, piece_width)
        for chip, owner in enumerate(owners):
            held = chip_rows(
                owner,
                far_refs[chip * pieces + piece].at[:, :, offset : offset + tile],
                far_refs[(chips + chip) * pieces + piece].at[:, :, offset : offset + tile],
            )
            both = both + dot(chip_table(table_ref, owner, rows), held)
        src_re, src_im = both[:bins, :tile], both[bins:, :tile]
        grad_re, grad_im = both[:bins, tile:], both[bins:, tile:]
        filt_re, filt_im = filt_ref[:bins, there], filt_ref[bins:, there]
        real = [
            src_re * filt_re - src_im * filt_im,
            filt_re * grad_re + filt_im * grad_im,
            src_re * grad_re + src_im * grad_im,
        ]
        imag = [
            src_re * filt_im + src_im * filt_re,
            filt_re * grad_im - filt_im * grad_re,
            src_re * grad_im - src_im * grad_re,
        ]
        products = jnp.concatenate(
            [
                jnp.concatenate([re.astype(BF16), im.astype(BF16)], axis=0)
                for re, im in zip(real, imag)
            ],
            axis=1,
        )
        result = dot(back_ref[...], products)
        conv_out, grad_source = result[:, :tile], result[:, tile : 2 * tile]
        gfilt[:, here] = result[:, 2 * tile :]
        gated[:, here] = (proj_ref[1, :, there].astype(F32) * conv_out).astype(BF16)
        gproj[0, :, here] = (grad_source * proj_ref[2, :, there].astype(F32)).astype(BF16)
        gproj[1, :, here] = (grad_ref[:, there].astype(F32) * conv_out).astype(BF16)
        gproj[2, :, here] = (grad_source * proj_ref[0, :, there].astype(F32)).astype(BF16)
        number = start // tile
        copies += [
            pltpu.make_async_copy(gated.at[:, here], gated_out.at[:, there], sems.at[number, 0]),
            pltpu.make_async_copy(gproj.at[:, :, here], gproj_out.at[:, :, there], sems.at[number, 1]),
            pltpu.make_async_copy(gfilt.at[:, here], gfilt_out.at[:, there], sems.at[number, 2]),
        ]
        for copy in copies[-3:]:
            copy.start()
    for copy in copies:
        copy.wait()


def convolve(device, chans, groups, table, back, grad_out, proj, filt, near, far, pieces, outs, cut):
    rows, width = grad_out.shape
    bins, length = table.shape
    chunk_width = cut.stop - cut.start
    chips = groups // 2 - 1
    tile = divisor(chunk_width, 256)
    operands = [device, table, back, grad_out, proj, filt, near, *far]
    in_specs = [SMEM] + [VMEM] * (len(operands) - 1)
    aliases = {}
    if outs:
        aliases = {len(operands) + i: i for i in range(3)}
        in_specs += [ANY] * 3
        operands += outs
    size = 48 * length * tile + 20 * chips * rows * chunk_width + 2 * table.size + 2**22
    return pl.pallas_call(
        functools.partial(conv_kernel, chans, groups, pieces, cut.start, tile, bool(outs)),
        in_specs=in_specs,
        out_specs=[ANY] * 3,
        out_shape=[
            jax.ShapeDtypeStruct((rows, width), BF16),
            jax.ShapeDtypeStruct((3, rows, width), BF16),
            jax.ShapeDtypeStruct((rows, width), F32),
        ],
        scratch_shapes=[
            pltpu.VMEM((rows, chunk_width), BF16),
            pltpu.VMEM((3, rows, chunk_width), BF16),
            pltpu.VMEM((rows, chunk_width), F32),
            pltpu.SemaphoreType.DMA((chunk_width // tile, 3)),
        ],
        input_output_aliases=aliases,
        compiler_params=params(mebibytes_for(size)),
        cost_estimate=pl.CostEstimate(flops=2**20, bytes_accessed=2**16, transcendentals=0),
        name="convolve",
    )(*operands)


def to_other_core(value, groups):
    return lax.ppermute(value, "seq", [(i, i ^ 1) for i in range(groups)])


def from_other_chips(value, groups):
    return [
        lax.ppermute(value, "seq", [(i, (i + 2 * d) % groups) for i in range(groups)])
        for d in range(1, groups // 2)
    ]


def per_device(tokens, in_weight, long_filter, grad_out):
    rows, width = long_filter.shape
    depth = tokens.shape[1]
    groups = lax.axis_size("seq")
    chans = lax.axis_size("chan")
    seq_index = lax.axis_index("seq")
    chan_index = lax.axis_index("chan")
    length = rows * groups
    weight = jnp.transpose(in_weight, (1, 0, 2))

    device = (seq_index * chans + chan_index)[None]
    forward = ring_pairs(chans)
    reverse = [(b, a) for a, b in forward]
    steps = chans // 2

    up, down = tokens, tokens
    total, first, x = None, None, pltpu.with_memory_space_constraint(tokens, pltpu.HBM)
    for step in range(1, steps + 1):
        next_up = lax.ppermute(up, "chan", forward)
        if step < steps:
            next_down = lax.ppermute(down, "chan", reverse)
        offsets = (step - 1, -step)
        taps = []
        if step > 1:
            total, weights = add_blocks(device, chans, offsets, total, first, x, weight)
        else:
            filt = pltpu.with_memory_space_constraint(long_filter, pltpu.HBM)
            total, weights, filt = add_blocks(device, chans, offsets, None, None, x, weight, filt)
            filters = [filt] + from_other_chips(filt, groups)
        if step == 2:
            taps = filters
        if step < steps:
            up, down, total, *taps = lax.optimization_barrier((next_up, next_down, total, *taps))
            filters = taps or filters
            first, x = (up, in_vmem(weights)), down
        else:
            last, total = lax.optimization_barrier((next_up, total))
    taps = filters

    table = transform_table(length)
    edge = width // 2
    pieces = [slice(0, edge), slice(edge, width)] if edge % 256 == 0 else [slice(0, width)]
    proj, pair, *parts = last_block(total, grad_out, last, weights, pieces)
    far = from_other_chips(pair, groups)
    taps = taps + [to_other_core(block, groups) for block in taps]
    others = [to_other_core(part, groups) for part in parts]
    filt, near, back = spectra(device, chans, table, taps, pair, others)
    *far, near = lax.optimization_barrier((*far, near))
    far = far + [to_other_core(block, groups) for block in far]
    outs = convolve(
        device, chans, groups, table, back, grad_out, proj, filt, near, far, 1, None, slice(0, width)
    )
    gated_out, grad_proj, grad_filter = outs
    return gated_out, jnp.transpose(grad_proj, (1, 0, 2)), grad_filter


def solution(mesh):
    in_specs = (P("seq", "chan"), P(None, None, "chan"), P("seq", "chan"), P("seq", "chan"))
    out_specs = (P("seq", "chan"), P("seq", None, "chan"), P("seq", "chan"))
    return jax.shard_map(
        per_device, mesh=mesh, in_specs=in_specs, out_specs=out_specs, check_vma=False
    )
```

```python
import functools

import jax
import jax.numpy as jnp
import numpy as np
from jax import lax
from jax.experimental import pallas as pl
from jax.experimental.pallas import tpu as pltpu
from jax.sharding import PartitionSpec as P

BF16 = jnp.bfloat16
F32 = jnp.float32


def dot(a, b):
    return jnp.dot(a, b, preferred_element_type=F32)


def divisor(size, most):
    tile = min(size, most)
    while size % tile:
        tile //= 2
    return tile


def params(mebibytes):
    return pltpu.CompilerParams(vmem_limit_bytes=mebibytes * 1024 * 1024)


def mebibytes_for(size):
    return max(8, -(-size // 2**20) + 4)


def ring_order(size):
    evens = list(range(0, size, 2))
    return evens + [index + 1 for index in reversed(evens)]


def ring_pairs(size):
    order = ring_order(size)
    return [(order[i], order[(i + 1) % size]) for i in range(size)]


def remainder(number, size):
    return number & (size - 1) if size & (size - 1) == 0 else lax.rem(number, size)


def quotient(number, size):
    return number >> (size.bit_length() - 1) if size & (size - 1) == 0 else lax.div(number, size)


def ring_owner(device, chans, offset):
    index = remainder(device, chans)
    half = index >> 1
    position = jnp.where(index & 1 == 0, half, chans - 1 - half)
    position = remainder(position + (offset + chans), chans)
    return jnp.where(position < chans // 2, 2 * position, 2 * (chans - 1 - position) + 1)


def sequence_owner(device, chans, groups, distance):
    return remainder(quotient(device, chans) + (groups - 2 * distance), groups)


def in_vmem(array):
    return pltpu.with_memory_space_constraint(array, pltpu.VMEM)


SPARE = 16
VMEM = pl.BlockSpec(memory_space=pltpu.VMEM)
SMEM = pl.BlockSpec(memory_space=pltpu.SMEM)
ANY = pl.BlockSpec(memory_space=pl.ANY)
HBM = pl.BlockSpec(memory_space=pltpu.HBM)


def blocks_kernel(chans, offsets, first, fresh, own, device_ref, *refs):
    first_refs, refs = (refs[:2], refs[2:]) if first else ((), refs)
    total_ref, refs = (None, refs) if fresh else (refs[0], refs[1:])
    if own:
        x_ref, source, filter_ref, out_ref, next_ref, filt_ref, held, sems, *own_refs = refs
        own_x, own_filter, own_sems = own_refs
        own_copies = [
            pltpu.make_async_copy(x_ref, own_x, own_sems.at[0]),
            pltpu.make_async_copy(filter_ref, own_filter, own_sems.at[1]),
        ]
        own_copies[0].start()
        x_ref = own_x
    else:
        x_ref, source, out_ref, next_ref, held, sems = refs
    depth = x_ref.shape[1]
    copies = []
    for slot, target in enumerate((held, next_ref)):
        start = pl.multiple_of(ring_owner(device_ref[0], chans, offsets[slot]) * depth, depth)
        copies.append(
            pltpu.make_async_copy(source.at[:, pl.ds(start, depth)], target, sems.at[slot])
        )
        copies[slot].start()
    if own:
        own_copies[1].start()
    values = [None if fresh else total_ref[j] for j in range(3)]
    if first:
        for j in range(3):
            part = dot(first_refs[0][...], first_refs[1][j])
            values[j] = part if fresh else values[j] + part
            out_ref[j] = values[j]
    if own:
        own_copies[0].wait()
    copies[0].wait()
    for j in range(3):
        part = dot(x_ref[...], held[j])
        out_ref[j] = out_ref[j] + part if first else (part if fresh else values[j] + part)
    if own:
        own_copies[1].wait()
        rows = own_filter.shape[0]
        filt_ref[:rows] = own_filter[...].astype(BF16)
        filt_ref[rows:] = own_filter[: filt_ref.shape[0] - rows].astype(BF16)
    copies[1].wait()


def add_blocks(device, chans, offsets, total, first, x, weight, long_filter=None):
    rows, depth = x.shape
    width = weight.shape[2]
    own = first is None
    operands = [device, *(first or ())]
    aliases = {}
    if total is not None:
        aliases = {len(operands): 0}
        operands.append(total)
    operands += [x, weight] + [long_filter] * own
    block = (3, depth, width)
    size = 2 * int(np.prod(block)) + 16 * rows * width + 8 * rows * depth
    scratch = [pltpu.VMEM(block, BF16), pltpu.SemaphoreType.DMA((2,))]
    if own:
        size += 16 * rows * width
        scratch += [
            pltpu.VMEM((rows, depth), BF16),
            pltpu.VMEM((rows, width), F32),
            pltpu.SemaphoreType.DMA((2,)),
        ]
    return pl.pallas_call(
        functools.partial(blocks_kernel, chans, offsets, not own, total is None, own),
        in_specs=[SMEM] + ([ANY] * 3 if own else [VMEM] * (len(operands) - 2) + [ANY]),
        out_specs=[VMEM] * (2 + own),
        out_shape=[jax.ShapeDtypeStruct((3, rows, width), F32), pltpu.VMEM(block, BF16)]
        + [jax.ShapeDtypeStruct((rows + SPARE, width), BF16)] * own,
        scratch_shapes=scratch,
        input_output_aliases=aliases,
        compiler_params=params(mebibytes_for(size)),
        cost_estimate=pl.CostEstimate(
            flops=12 * rows * depth * width, bytes_accessed=12 * depth * width, transcendentals=0
        ),
        name="add_blocks",
    )(*operands)


def last_kernel(cuts, total_ref, grad_ref, x_ref, weight_ref, proj_ref, whole_ref, *piece_refs):
    for piece_ref, columns in zip(piece_refs, cuts):
        streams = []
        for j in range(3):
            value = total_ref[j, :, columns] + dot(x_ref[...], weight_ref[j, :, columns])
            value = value.astype(BF16)
            proj_ref[j, :, columns] = value
            streams.append(value.astype(F32))
        source = (streams[0] * streams[2]).astype(BF16)
        grad = (grad_ref[:, columns].astype(F32) * streams[1]).astype(BF16)
        for ref, place in ((whole_ref, columns), (piece_ref, slice(None))):
            ref[0, :, place] = source
            ref[1, :, place] = grad


def last_block(total, grad_out, x, weights, cuts):
    rows, width = grad_out.shape
    depth = x.shape[1]
    size = 40 * rows * width + 4 * rows * depth
    return pl.pallas_call(
        functools.partial(last_kernel, cuts),
        in_specs=[VMEM] * 4,
        out_specs=[VMEM] * (2 + len(cuts)),
        out_shape=[pltpu.VMEM((3, rows, width), BF16), pltpu.VMEM((2, rows, width), BF16)]
        + [pltpu.VMEM((2, rows, cut.stop - cut.start), BF16) for cut in cuts],
        compiler_params=params(mebibytes_for(size)),
        cost_estimate=pl.CostEstimate(
            flops=6 * rows * depth * width, bytes_accessed=2**20, transcendentals=0
        ),
        name="last_block",
    )(total, grad_out, x, in_vmem(weights))


def transform_table(length):
    steps = np.arange(length)
    turns = np.outer(2 * steps + 1, steps) % (4 * length)
    angle = turns * (np.pi / (2 * length))
    table = np.concatenate([np.cos(angle), -np.sin(angle)], axis=0).astype(np.float32)
    return jnp.asarray(table.astype(jnp.bfloat16))


def chip_rows(owner, ref, other_ref):
    first = owner & 1 == 0
    signals = []
    for signal in range(2):
        mine, others = ref[signal], other_ref[signal]
        signals.append(
            jnp.concatenate([jnp.where(first, mine, others), jnp.where(first, others, mine)], axis=0)
        )
    return jnp.concatenate(signals, axis=1)


def chip_table(table_ref, owner, rows):
    return table_ref[:, pl.ds(pl.multiple_of((owner >> 1) * (2 * rows), 256), 2 * rows)]


def spectra_kernel(chans, groups, device_ref, table_ref, *refs):
    tap_refs, (own_ref, *other_refs) = refs[:groups], refs[groups:-4]
    filt_ref, near_ref, back_ref, taps = refs[-4:]
    rows, width = own_ref.shape[1:]
    tile = divisor(width, 256)
    chips = groups // 2
    for number, ref in enumerate(tap_refs):
        owner = sequence_owner(device_ref[0], chans, groups, number % chips)
        if number >= chips:
            owner = owner ^ 1
        taps[pl.ds(pl.multiple_of(owner * rows, 128), rows)] = ref[:rows]
    for start in range(0, width, tile):
        columns = slice(start, start + tile)
        filt_ref[:, columns] = dot(table_ref[...], taps[:, columns])
    owner = sequence_owner(device_ref[0], chans, groups, 0)
    length = table_ref.shape[1]
    mine = table_ref[:, pl.ds(pl.multiple_of(owner * rows, 128), rows)]
    back_ref[...] = (mine.astype(F32).T * (1.0 / length)).astype(BF16)
    table = chip_table(table_ref, owner, rows)
    for start in range(0, width, tile):
        piece, offset = divmod(start, other_refs[0].shape[2])
        held = chip_rows(
            owner,
            own_ref.at[:, :, start : start + tile],
            other_refs[piece].at[:, :, offset : offset + tile],
        )
        near_ref[:, 2 * start : 2 * start + 2 * tile] = dot(table, held)


def spectra(device, chans, table, taps, pair, other_pieces):
    rows, width = pair.shape[1:]
    bins, length = table.shape
    size = 2 * table.size + 4 * length * width + 40 * rows * width + 2**21
    return pl.pallas_call(
        functools.partial(spectra_kernel, chans, len(taps)),
        in_specs=[SMEM] + [VMEM] * (2 + len(taps) + len(other_pieces)),
        out_specs=[VMEM] * 3,
        out_shape=[
            pltpu.VMEM((bins, width), F32),
            pltpu.VMEM((bins, 2 * width), F32),
            pltpu.VMEM((rows, bins), BF16),
        ],
        scratch_shapes=[pltpu.VMEM((length, width), BF16)],
        compiler_params=params(mebibytes_for(size)),
        cost_estimate=pl.CostEstimate(flops=2**20, bytes_accessed=2**16, transcendentals=0),
        name="spectra",
    )(device, table, *taps, pair, *other_pieces)


def conv_kernel(chans, groups, pieces, first, tile, aliased, device_ref, *refs):
    chips = groups // 2 - 1
    table_ref, back_ref, grad_ref, proj_ref, filt_ref, near_ref, *refs = refs
    count = 2 * chips * pieces
    far_refs, refs = refs[:count], refs[count + 3 * aliased :]
    gated_out, gproj_out, gfilt_out, gated, gproj, gfilt, sems = refs
    rows, width = gated.shape
    bins = table_ref.shape[0] // 2
    owners = [sequence_owner(device_ref[0], chans, groups, chip + 1) for chip in range(chips)]
    piece_width = width // pieces
    copies = []
    for start in range(0, width, tile):
        here = slice(start, start + tile)
        there = slice(first + start, first + start + tile)
        pairs = slice(2 * (first + start), 2 * (first + start) + 2 * tile)
        both = near_ref[:, pairs]
        piece, offset = divmod(start, piece_width)
        for chip, owner in enumerate(owners):
            held = chip_rows(
                owner,
                far_refs[chip * pieces + piece].at[:, :, offset : offset + tile],
                far_refs[(chips + chip) * pieces + piece].at[:, :, offset : offset + tile],
            )
            both = both + dot(chip_table(table_ref, owner, rows), held)
        src_re, src_im = both[:bins, :tile], both[bins:, :tile]
        grad_re, grad_im = both[:bins, tile:], both[bins:, tile:]
        filt_re, filt_im = filt_ref[:bins, there], filt_ref[bins:, there]
        real = [
            src_re * filt_re - src_im * filt_im,
            filt_re * grad_re + filt_im * grad_im,
            src_re * grad_re + src_im * grad_im,
        ]
        imag = [
            src_re * filt_im + src_im * filt_re,
            filt_re * grad_im - filt_im * grad_re,
            src_re * grad_im - src_im * grad_re,
        ]
        products = jnp.concatenate(
            [
                jnp.concatenate([re.astype(BF16), im.astype(BF16)], axis=0)
                for re, im in zip(real, imag)
            ],
            axis=1,
        )
        result = dot(back_ref[...], products)
        conv_out, grad_source = result[:, :tile], result[:, tile : 2 * tile]
        gfilt[:, here] = result[:, 2 * tile :]
        gated[:, here] = (proj_ref[1, :, there].astype(F32) * conv_out).astype(BF16)
        gproj[0, :, here] = (grad_source * proj_ref[2, :, there].astype(F32)).astype(BF16)
        gproj[1, :, here] = (grad_ref[:, there].astype(F32) * conv_out).astype(BF16)
        gproj[2, :, here] = (grad_source * proj_ref[0, :, there].astype(F32)).astype(BF16)
        number = start // tile
        copies += [
            pltpu.make_async_copy(gated.at[:, here], gated_out.at[:, there], sems.at[number, 0]),
            pltpu.make_async_copy(gproj.at[:, :, here], gproj_out.at[:, :, there], sems.at[number, 1]),
            pltpu.make_async_copy(gfilt.at[:, here], gfilt_out.at[:, there], sems.at[number, 2]),
        ]
        for copy in copies[-3:]:
            copy.start()
    for copy in copies:
        copy.wait()


def convolve(device, chans, groups, table, back, grad_out, proj, filt, near, far, pieces, outs, cut):
    rows, width = grad_out.shape
    bins, length = table.shape
    chunk_width = cut.stop - cut.start
    chips = groups // 2 - 1
    tile = divisor(chunk_width, 256)
    operands = [device, table, back, grad_out, proj, filt, near, *far]
    in_specs = [SMEM] + [VMEM] * (len(operands) - 1)
    aliases = {}
    if outs:
        aliases = {len(operands) + i: i for i in range(3)}
        in_specs += [ANY] * 3
        operands += outs
    size = 48 * length * tile + 20 * chips * rows * chunk_width + 2 * table.size + 2**22
    return pl.pallas_call(
        functools.partial(conv_kernel, chans, groups, pieces, cut.start, tile, bool(outs)),
        in_specs=in_specs,
        out_specs=[ANY] * 3,
        out_shape=[
            jax.ShapeDtypeStruct((rows, width), BF16),
            jax.ShapeDtypeStruct((3, rows, width), BF16),
            jax.ShapeDtypeStruct((rows, width), F32),
        ],
        scratch_shapes=[
            pltpu.VMEM((rows, chunk_width), BF16),
            pltpu.VMEM((3, rows, chunk_width), BF16),
            pltpu.VMEM((rows, chunk_width), F32),
            pltpu.SemaphoreType.DMA((chunk_width // tile, 3)),
        ],
        input_output_aliases=aliases,
        compiler_params=params(mebibytes_for(size)),
        cost_estimate=pl.CostEstimate(flops=2**20, bytes_accessed=2**16, transcendentals=0),
        name="convolve",
    )(*operands)


def to_other_core(value, groups):
    return lax.ppermute(value, "seq", [(i, i ^ 1) for i in range(groups)])


def from_other_chips(value, groups):
    return [
        lax.ppermute(value, "seq", [(i, (i + 2 * d) % groups) for i in range(groups)])
        for d in range(1, groups // 2)
    ]


def per_device(tokens, in_weight, long_filter, grad_out):
    rows, width = long_filter.shape
    depth = tokens.shape[1]
    groups = lax.axis_size("seq")
    chans = lax.axis_size("chan")
    seq_index = lax.axis_index("seq")
    chan_index = lax.axis_index("chan")
    length = rows * groups
    weight = jnp.transpose(in_weight, (1, 0, 2))

    device = (seq_index * chans + chan_index)[None]
    forward = ring_pairs(chans)
    reverse = [(b, a) for a, b in forward]
    steps = chans // 2

    up, down = tokens, tokens
    total, first, x = None, None, pltpu.with_memory_space_constraint(tokens, pltpu.HBM)
    for step in range(1, steps + 1):
        next_up = lax.ppermute(up, "chan", forward)
        if step < steps:
            next_down = lax.ppermute(down, "chan", reverse)
        offsets = (step - 1, -step)
        taps = []
        if step > 1:
            total, weights = add_blocks(device, chans, offsets, total, first, x, weight)
        else:
            filt = pltpu.with_memory_space_constraint(long_filter, pltpu.HBM)
            total, weights, filt = add_blocks(device, chans, offsets, None, None, x, weight, filt)
            filters = [filt] + from_other_chips(filt, groups)
        if step == 2:
            taps = filters
        if step < steps:
            up, down, total, *taps = lax.optimization_barrier((next_up, next_down, total, *taps))
            filters = taps or filters
            first, x = (up, in_vmem(weights)), down
        else:
            last, total = lax.optimization_barrier((next_up, total))
    taps = filters

    table = transform_table(length)
    edge = width // 2
    pieces = [slice(0, edge), slice(edge, width)] if edge % 256 == 0 else [slice(0, width)]
    proj, pair, *parts = last_block(total, grad_out, last, weights, pieces)
    far = from_other_chips(pair, groups)
    taps = taps + [to_other_core(block, groups) for block in taps]
    others = [to_other_core(part, groups) for part in parts]
    filt, near, back = spectra(device, chans, table, taps, pair, others)
    *far, near = lax.optimization_barrier((*far, near))
    far = far + [to_other_core(block, groups) for block in far]
    outs = convolve(
        device, chans, groups, table, back, grad_out, proj, filt, near, far, 1, None, slice(0, width)
    )
    gated_out, grad_proj, grad_filter = outs
    return gated_out, jnp.transpose(grad_proj, (1, 0, 2)), grad_filter


def solution(mesh):
    in_specs = (P("seq", "chan"), P(None, None, "chan"), P("seq", "chan"), P("seq", "chan"))
    out_specs = (P("seq", "chan"), P("seq", None, "chan"), P("seq", "chan"))
    return jax.shard_map(
        per_device, mesh=mesh, in_specs=in_specs, out_specs=out_specs, check_vma=False
    )
```

```python
import functools

import jax
import jax.numpy as jnp
import numpy as np
from jax import lax
from jax.experimental import pallas as pl
from jax.experimental.pallas import tpu as pltpu
from jax.sharding import PartitionSpec as P

BF16 = jnp.bfloat16
F32 = jnp.float32


def dot(a, b):
    return jnp.dot(a, b, preferred_element_type=F32)


def divisor(size, most):
    tile = min(size, most)
    while size % tile:
        tile //= 2
    return tile


def params(mebibytes):
    return pltpu.CompilerParams(vmem_limit_bytes=mebibytes * 1024 * 1024)


def mebibytes_for(size):
    return max(8, -(-size // 2**20) + 4)


def ring_order(size):
    evens = list(range(0, size, 2))
    return evens + [index + 1 for index in reversed(evens)]


def ring_pairs(size):
    order = ring_order(size)
    return [(order[i], order[(i + 1) % size]) for i in range(size)]


def remainder(number, size):
    return number & (size - 1) if size & (size - 1) == 0 else lax.rem(number, size)


def quotient(number, size):
    return number >> (size.bit_length() - 1) if size & (size - 1) == 0 else lax.div(number, size)


def ring_owner(device, chans, offset):
    index = remainder(device, chans)
    half = index >> 1
    position = jnp.where(index & 1 == 0, half, chans - 1 - half)
    position = remainder(position + (offset + chans), chans)
    return jnp.where(position < chans // 2, 2 * position, 2 * (chans - 1 - position) + 1)


def sequence_owner(device, chans, groups, distance):
    return remainder(quotient(device, chans) + (groups - 2 * distance), groups)


def in_vmem(array):
    return pltpu.with_memory_space_constraint(array, pltpu.VMEM)


SPARE = 16
VMEM = pl.BlockSpec(memory_space=pltpu.VMEM)
SMEM = pl.BlockSpec(memory_space=pltpu.SMEM)
ANY = pl.BlockSpec(memory_space=pl.ANY)
HBM = pl.BlockSpec(memory_space=pltpu.HBM)


def blocks_kernel(chans, offsets, first, fresh, own, device_ref, *refs):
    first_refs, refs = (refs[:2], refs[2:]) if first else ((), refs)
    total_ref, refs = (None, refs) if fresh else (refs[0], refs[1:])
    if own:
        x_ref, source, filter_ref, out_ref, next_ref, filt_ref, held, sems, *own_refs = refs
        own_x, own_filter, own_sems = own_refs
        own_copies = [
            pltpu.make_async_copy(x_ref, own_x, own_sems.at[0]),
            pltpu.make_async_copy(filter_ref, own_filter, own_sems.at[1]),
        ]
        own_copies[0].start()
        x_ref = own_x
    else:
        x_ref, source, out_ref, next_ref, held, sems = refs
    depth = x_ref.shape[1]
    copies = []
    for slot, target in enumerate((held, next_ref)):
        start = pl.multiple_of(ring_owner(device_ref[0], chans, offsets[slot]) * depth, depth)
        copies.append(
            pltpu.make_async_copy(source.at[:, pl.ds(start, depth)], target, sems.at[slot])
        )
        copies[slot].start()
    if own:
        own_copies[1].start()
    values = [None if fresh else total_ref[j] for j in range(3)]
    if first:
        for j in range(3):
            part = dot(first_refs[0][...], first_refs[1][j])
            values[j] = part if fresh else values[j] + part
            out_ref[j] = values[j]
    if own:
        own_copies[0].wait()
    copies[0].wait()
    for j in range(3):
        part = dot(x_ref[...], held[j])
        out_ref[j] = out_ref[j] + part if first else (part if fresh else values[j] + part)
    if own:
        own_copies[1].wait()
        rows = own_filter.shape[0]
        filt_ref[:rows] = own_filter[...].astype(BF16)
        filt_ref[rows:] = own_filter[: filt_ref.shape[0] - rows].astype(BF16)
    copies[1].wait()


def add_blocks(device, chans, offsets, total, first, x, weight, long_filter=None):
    rows, depth = x.shape
    width = weight.shape[2]
    own = first is None
    operands = [device, *(first or ())]
    aliases = {}
    if total is not None:
        aliases = {len(operands): 0}
        operands.append(total)
    operands += [x, weight] + [long_filter] * own
    block = (3, depth, width)
    size = 2 * int(np.prod(block)) + 16 * rows * width + 8 * rows * depth
    scratch = [pltpu.VMEM(block, BF16), pltpu.SemaphoreType.DMA((2,))]
    if own:
        size += 16 * rows * width
        scratch += [
            pltpu.VMEM((rows, depth), BF16),
            pltpu.VMEM((rows, width), F32),
            pltpu.SemaphoreType.DMA((2,)),
        ]
    return pl.pallas_call(
        functools.partial(blocks_kernel, chans, offsets, not own, total is None, own),
        in_specs=[SMEM] + ([ANY] * 3 if own else [VMEM] * (len(operands) - 2) + [ANY]),
        out_specs=[VMEM] * (2 + own),
        out_shape=[jax.ShapeDtypeStruct((3, rows, width), F32), pltpu.VMEM(block, BF16)]
        + [jax.ShapeDtypeStruct((rows + SPARE, width), BF16)] * own,
        scratch_shapes=scratch,
        input_output_aliases=aliases,
        compiler_params=params(mebibytes_for(size)),
        cost_estimate=pl.CostEstimate(
            flops=12 * rows * depth * width, bytes_accessed=12 * depth * width, transcendentals=0
        ),
        name="add_blocks",
    )(*operands)


def last_kernel(cuts, total_ref, grad_ref, x_ref, weight_ref, proj_ref, whole_ref, *piece_refs):
    for piece_ref, columns in zip(piece_refs, cuts):
        streams = []
        for j in range(3):
            value = total_ref[j, :, columns] + dot(x_ref[...], weight_ref[j, :, columns])
            value = value.astype(BF16)
            proj_ref[j, :, columns] = value
            streams.append(value.astype(F32))
        source = (streams[0] * streams[2]).astype(BF16)
        grad = (grad_ref[:, columns].astype(F32) * streams[1]).astype(BF16)
        for ref, place in ((whole_ref, columns), (piece_ref, slice(None))):
            ref[0, :, place] = source
            ref[1, :, place] = grad


def last_block(total, grad_out, x, weights, cuts):
    rows, width = grad_out.shape
    depth = x.shape[1]
    size = 40 * rows * width + 4 * rows * depth
    return pl.pallas_call(
        functools.partial(last_kernel, cuts),
        in_specs=[VMEM] * 4,
        out_specs=[VMEM] * (2 + len(cuts)),
        out_shape=[pltpu.VMEM((3, rows, width), BF16), pltpu.VMEM((2, rows, width), BF16)]
        + [pltpu.VMEM((2, rows, cut.stop - cut.start), BF16) for cut in cuts],
        compiler_params=params(mebibytes_for(size)),
        cost_estimate=pl.CostEstimate(
            flops=6 * rows * depth * width, bytes_accessed=2**20, transcendentals=0
        ),
        name="last_block",
    )(total, grad_out, x, in_vmem(weights))


def transform_table(length):
    steps = np.arange(length)
    turns = np.outer(2 * steps + 1, steps) % (4 * length)
    angle = turns * (np.pi / (2 * length))
    table = np.concatenate([np.cos(angle), -np.sin(angle)], axis=0).astype(np.float32)
    return jnp.asarray(table.astype(jnp.bfloat16))


def chip_rows(owner, ref, other_ref):
    first = owner & 1 == 0
    signals = []
    for signal in range(2):
        mine, others = ref[signal], other_ref[signal]
        signals.append(
            jnp.concatenate([jnp.where(first, mine, others), jnp.where(first, others, mine)], axis=0)
        )
    return jnp.concatenate(signals, axis=1)


def chip_table(table_ref, owner, rows):
    return table_ref[:, pl.ds(pl.multiple_of((owner >> 1) * (2 * rows), 256), 2 * rows)]


def spectra_kernel(chans, groups, device_ref, table_ref, *refs):
    tap_refs, (own_ref, *other_refs) = refs[:groups], refs[groups:-4]
    filt_ref, near_ref, back_ref, taps = refs[-4:]
    rows, width = own_ref.shape[1:]
    tile = divisor(width, 256)
    chips = groups // 2
    for number, ref in enumerate(tap_refs):
        owner = sequence_owner(device_ref[0], chans, groups, number % chips)
        if number >= chips:
            owner = owner ^ 1
        taps[pl.ds(pl.multiple_of(owner * rows, 128), rows)] = ref[:rows]
    for start in range(0, width, tile):
        columns = slice(start, start + tile)
        filt_ref[:, columns] = dot(table_ref[...], taps[:, columns])
    owner = sequence_owner(device_ref[0], chans, groups, 0)
    length = table_ref.shape[1]
    mine = table_ref[:, pl.ds(pl.multiple_of(owner * rows, 128), rows)]
    back_ref[...] = (mine.astype(F32).T * (1.0 / length)).astype(BF16)
    table = chip_table(table_ref, owner, rows)
    for start in range(0, width, tile):
        piece, offset = divmod(start, other_refs[0].shape[2])
        held = chip_rows(
            owner,
            own_ref.at[:, :, start : start + tile],
            other_refs[piece].at[:, :, offset : offset + tile],
        )
        near_ref[:, 2 * start : 2 * start + 2 * tile] = dot(table, held)


def spectra(device, chans, table, taps, pair, other_pieces):
    rows, width = pair.shape[1:]
    bins, length = table.shape
    size = 2 * table.size + 4 * length * width + 40 * rows * width + 2**21
    return pl.pallas_call(
        functools.partial(spectra_kernel, chans, len(taps)),
        in_specs=[SMEM] + [VMEM] * (2 + len(taps) + len(other_pieces)),
        out_specs=[VMEM] * 3,
        out_shape=[
            pltpu.VMEM((bins, width), F32),
            pltpu.VMEM((bins, 2 * width), F32),
            pltpu.VMEM((rows, bins), BF16),
        ],
        scratch_shapes=[pltpu.VMEM((length, width), BF16)],
        compiler_params=params(mebibytes_for(size)),
        cost_estimate=pl.CostEstimate(flops=2**20, bytes_accessed=2**16, transcendentals=0),
        name="spectra",
    )(device, table, *taps, pair, *other_pieces)


def conv_kernel(chans, groups, pieces, first, tile, aliased, device_ref, *refs):
    chips = groups // 2 - 1
    table_ref, back_ref, grad_ref, proj_ref, filt_ref, near_ref, *refs = refs
    count = 2 * chips * pieces
    far_refs, refs = refs[:count], refs[count + 3 * aliased :]
    gated_out, gproj_out, gfilt_out, gated, gproj, gfilt, sems = refs
    rows, width = gated.shape
    bins = table_ref.shape[0] // 2
    owners = [sequence_owner(device_ref[0], chans, groups, chip + 1) for chip in range(chips)]
    piece_width = width // pieces
    copies = []
    for start in range(0, width, tile):
        here = slice(start, start + tile)
        there = slice(first + start, first + start + tile)
        pairs = slice(2 * (first + start), 2 * (first + start) + 2 * tile)
        both = near_ref[:, pairs]
        piece, offset = divmod(start, piece_width)
        for chip, owner in enumerate(owners):
            held = chip_rows(
                owner,
                far_refs[chip * pieces + piece].at[:, :, offset : offset + tile],
                far_refs[(chips + chip) * pieces + piece].at[:, :, offset : offset + tile],
            )
            both = both + dot(chip_table(table_ref, owner, rows), held)
        src_re, src_im = both[:bins, :tile], both[bins:, :tile]
        grad_re, grad_im = both[:bins, tile:], both[bins:, tile:]
        filt_re, filt_im = filt_ref[:bins, there], filt_ref[bins:, there]
        number = start // tile

        def back(real, imag):
            products = jnp.concatenate([real.astype(BF16), imag.astype(BF16)], axis=0)
            return dot(back_ref[...], products)

        def send(source, target, output):
            copies.append(pltpu.make_async_copy(source, target, sems.at[number, output]))
            copies[-1].start()

        conv_out = back(src_re * filt_re - src_im * filt_im, src_re * filt_im + src_im * filt_re)
        gated[:, here] = (proj_ref[1, :, there].astype(F32) * conv_out).astype(BF16)
        gproj[1, :, here] = (grad_ref[:, there].astype(F32) * conv_out).astype(BF16)
        grad_source = back(
            filt_re * grad_re + filt_im * grad_im, filt_re * grad_im - filt_im * grad_re
        )
        gproj[0, :, here] = (grad_source * proj_ref[2, :, there].astype(F32)).astype(BF16)
        gproj[2, :, here] = (grad_source * proj_ref[0, :, there].astype(F32)).astype(BF16)
        send(gated.at[:, here], gated_out.at[:, there], 0)
        send(gproj.at[:, :, here], gproj_out.at[:, :, there], 1)
        gfilt[:, here] = back(
            src_re * grad_re + src_im * grad_im, src_re * grad_im - src_im * grad_re
        )
        send(gfilt.at[:, here], gfilt_out.at[:, there], 2)
    for copy in copies:
        copy.wait()


def convolve(device, chans, groups, table, back, grad_out, proj, filt, near, far, pieces, outs, cut):
    rows, width = grad_out.shape
    bins, length = table.shape
    chunk_width = cut.stop - cut.start
    chips = groups // 2 - 1
    tile = divisor(chunk_width, 256)
    operands = [device, table, back, grad_out, proj, filt, near, *far]
    in_specs = [SMEM] + [VMEM] * (len(operands) - 1)
    aliases = {}
    if outs:
        aliases = {len(operands) + i: i for i in range(3)}
        in_specs += [ANY] * 3
        operands += outs
    size = 48 * length * tile + 20 * chips * rows * chunk_width + 2 * table.size + 2**22
    return pl.pallas_call(
        functools.partial(conv_kernel, chans, groups, pieces, cut.start, tile, bool(outs)),
        in_specs=in_specs,
        out_specs=[ANY] * 3,
        out_shape=[
            jax.ShapeDtypeStruct((rows, width), BF16),
            jax.ShapeDtypeStruct((3, rows, width), BF16),
            jax.ShapeDtypeStruct((rows, width), F32),
        ],
        scratch_shapes=[
            pltpu.VMEM((rows, chunk_width), BF16),
            pltpu.VMEM((3, rows, chunk_width), BF16),
            pltpu.VMEM((rows, chunk_width), F32),
            pltpu.SemaphoreType.DMA((chunk_width // tile, 3)),
        ],
        input_output_aliases=aliases,
        compiler_params=params(mebibytes_for(size)),
        cost_estimate=pl.CostEstimate(flops=2**20, bytes_accessed=2**16, transcendentals=0),
        name="convolve",
    )(*operands)


def to_other_core(value, groups):
    return lax.ppermute(value, "seq", [(i, i ^ 1) for i in range(groups)])


def from_other_chips(value, groups):
    return [
        lax.ppermute(value, "seq", [(i, (i + 2 * d) % groups) for i in range(groups)])
        for d in range(1, groups // 2)
    ]


def per_device(tokens, in_weight, long_filter, grad_out):
    rows, width = long_filter.shape
    depth = tokens.shape[1]
    groups = lax.axis_size("seq")
    chans = lax.axis_size("chan")
    seq_index = lax.axis_index("seq")
    chan_index = lax.axis_index("chan")
    length = rows * groups
    weight = jnp.transpose(in_weight, (1, 0, 2))

    device = (seq_index * chans + chan_index)[None]
    forward = ring_pairs(chans)
    reverse = [(b, a) for a, b in forward]
    steps = chans // 2

    up, down = tokens, tokens
    total, first, x = None, None, pltpu.with_memory_space_constraint(tokens, pltpu.HBM)
    for step in range(1, steps + 1):
        next_up = lax.ppermute(up, "chan", forward)
        if step < steps:
            next_down = lax.ppermute(down, "chan", reverse)
        offsets = (step - 1, -step)
        taps = []
        if step > 1:
            total, weights = add_blocks(device, chans, offsets, total, first, x, weight)
        else:
            filt = pltpu.with_memory_space_constraint(long_filter, pltpu.HBM)
            total, weights, filt = add_blocks(device, chans, offsets, None, None, x, weight, filt)
            filters = [filt] + from_other_chips(filt, groups)
        if step == 2:
            taps = filters
        if step < steps:
            up, down, total, *taps = lax.optimization_barrier((next_up, next_down, total, *taps))
            filters = taps or filters
            first, x = (up, in_vmem(weights)), down
        else:
            last, total = lax.optimization_barrier((next_up, total))
    taps = filters

    table = transform_table(length)
    edge = width // 2
    pieces = [slice(0, edge), slice(edge, width)] if edge % 256 == 0 else [slice(0, width)]
    proj, pair, *parts = last_block(total, grad_out, last, weights, pieces)
    far = from_other_chips(pair, groups)
    taps = taps + [to_other_core(block, groups) for block in taps]
    others = [to_other_core(part, groups) for part in parts]
    filt, near, back = spectra(device, chans, table, taps, pair, others)
    *far, near = lax.optimization_barrier((*far, near))
    far = far + [to_other_core(block, groups) for block in far]
    outs = convolve(
        device, chans, groups, table, back, grad_out, proj, filt, near, far, 1, None, slice(0, width)
    )
    gated_out, grad_proj, grad_filter = outs
    return gated_out, jnp.transpose(grad_proj, (1, 0, 2)), grad_filter


def solution(mesh):
    in_specs = (P("seq", "chan"), P(None, None, "chan"), P("seq", "chan"), P("seq", "chan"))
    out_specs = (P("seq", "chan"), P("seq", None, "chan"), P("seq", "chan"))
    return jax.shard_map(
        per_device, mesh=mesh, in_specs=in_specs, out_specs=out_specs, check_vma=False
    )
```
